128 devices in a mesh: wide: 32 (over z, x, core), narrow: 4 (over y).
Axes of the slice: x: 4, y: 4, z: 4, core: 2. Of those that a mesh axis runs over, the one named last changes fastest.
Arguments:
- users: bfloat16 [262144, 128], P(('wide', 'narrow')), may hold values from -0.234375 to 0.234375
- confidence: bfloat16 [2048, 128, 512], P(('wide', 'narrow')), may hold values from 0 to 400, as said below
- item_lists: int32 [2048, 512], P(('wide', 'narrow')), may hold values from 0 to 1535
- block_counts: int32 [2048], P(('wide', 'narrow')), may hold values from 256 to 512, as said below
- requests: int32 [128, 512], P(('wide', 'narrow')), may hold values from 0 to 511
- hot_factors: float32 [1024, 128], replicated, may hold values from -6 to 6
- cold_factors: float32 [65536, 128], P(('wide', 'narrow')), may hold values from -6 to 6
Outputs:
- hot_solution: float32 [1024, 128], replicated
- cold_solution: float32 [65536, 128], P(('wide', 'narrow'))
The draws below stay inside these ranges and needn't reach their ends.
Inputs may be any that keep to these rules, and one draw needn't show every extreme that they name: `confidence`: zero where the user did not click the slot's item, else at least 2; slots at or beyond a block's count hold values that are not used. `block_counts`: the largest count, 512, occurs in every draw. `requests`: a row index within the owner's 512 cold items; entry o * 4 + j of device s's row is its j-th request to device o. `item_lists`: entries below 1024 are hot items; entry 1024 + o * 4 + j is the j-th row that the block's device asked of device o; repeats allowed.
All inputs are finite; a program needn't handle non-finite values.
Results may differ from the reference program's by a relative error of at most 0.0043.
Values may be sent and summed in bfloat16 or wider, within the bound.
A program may use at most 64 MiB of HBM per device.

```python
import math
import jax
import jax.numpy as jnp
from jax import lax

R = 128
UB = 128
LM = 512
NB = 16
HOT = 1024
CAP = 4
COLD_DEV = 512
ITERS = 2
USERS = 262144
BLOCKS = 2048
COLD = 65536
SLOTS = 1536
N_WIDE = 32
N_NARROW = 4


def draw_users(key, part):
    key = jax.random.fold_in(key, 1)
    keys = jax.random.split(key, 3)
    row_scale = jnp.exp(jax.random.uniform(keys[1], (USERS, 1), jnp.float32, 0.0, math.log(10.0)))
    col_scale = jnp.exp(jax.random.uniform(keys[2], (1, R), jnp.float32, 0.0, math.log(10.0)))
    base = jnp.clip(jax.random.normal(keys[0], (USERS, R), jnp.float32), -4.0, 4.0)
    return (base * row_scale * col_scale * (0.3 / math.sqrt(USERS))).astype(jnp.bfloat16)


def draw_confidence(key, part):
    key = jax.random.fold_in(key, 2)
    keys = jax.random.split(key, 2)
    clicked = jax.random.randint(keys[0], (BLOCKS, UB, LM), 0, 2).astype(jnp.float32)
    level = jnp.exp(jax.random.uniform(keys[1], (BLOCKS, UB, LM), jnp.float32, math.log(2.0), math.log(400.0)))
    return (clicked * level).astype(jnp.bfloat16)


def draw_block_counts(key, part):
    key = jax.random.fold_in(key, 3)
    counts = jax.random.randint(key, (BLOCKS,), LM // 2, LM + 1)
    return counts.at[0].set(LM)


def plant(array, stream_key, low, high):
    index_at = [jax.random.randint(jax.random.fold_in(stream_key, axis), (), 0, length) for axis, length in enumerate(array.shape)]
    widest = array.shape.index(max(array.shape))
    beside = index_at[:widest] + [(index_at[widest] + 1) % array.shape[widest]] + index_at[widest + 1:]
    return array.at[tuple(index_at)].set(low).at[tuple(beside)].set(high)


def level_of(stream_key, dims, cuts, smallest, high):
    loudness = 1.0
    for axis_at, shards_of in cuts:
        draws = jax.random.uniform(jax.random.fold_in(jax.random.fold_in(stream_key, 6), axis_at), (shards_of,), jnp.float32, smallest / len(cuts), high / len(cuts))
        loudness = loudness * jnp.repeat(jnp.exp(draws), dims[axis_at] // shards_of).reshape((-1,) + (1,) * (len(dims) - 1 - axis_at))
    return loudness


def centred(stream_key, dims, spread, bound, cuts=(), kind=jnp.bfloat16):
    array = jax.random.normal(stream_key, dims, jnp.float32) * spread
    if len(cuts) > 0:
        array = level_of(stream_key, dims, cuts, -0.22, 0.18) * array
    return jnp.clip(array, min=-bound, max=bound).astype(kind)


def setup_inputs(seed: int = 0) -> dict:
    streams_of = jax.random.split(jax.random.key(seed), 8)
    return {
        "users": draw_users(jax.random.fold_in(streams_of[7], 71), 0),
        "confidence": draw_confidence(jax.random.fold_in(streams_of[7], 71), 0),
        "item_lists": plant(jax.random.randint(streams_of[2], (BLOCKS, LM), 0, SLOTS), jax.random.fold_in(streams_of[2], 1), 0, SLOTS - 1).astype(jnp.int32),
        "block_counts": draw_block_counts(jax.random.fold_in(streams_of[7], 71), 0),
        "requests": plant(jax.random.randint(streams_of[4], (N_WIDE * N_NARROW, N_WIDE * N_NARROW * CAP), 0, COLD_DEV), jax.random.fold_in(streams_of[4], 1), 0, COLD_DEV - 1).astype(jnp.int32),
        "hot_factors": centred(streams_of[5], (HOT, R), 1.0, 6.0, (), jnp.float32),
        "cold_factors": centred(streams_of[6], (COLD, R), 1.0, 6.0, ((0, 128),), jnp.float32),
    }


REGULAR = 1.0
EPS = 1e-6


def block_terms(rows, level_in, lists, counts, table, with_rhs):
    picked = table[lists]
    scores = jnp.einsum("bur,blr->bul", rows.astype(jnp.float32), picked.astype(jnp.float32))
    level = level_in.astype(jnp.float32)
    places = jnp.arange(lists.shape[1], dtype=jnp.int32)
    valid = (places[None, :] < counts[:, None]).astype(jnp.float32)[:, None, :]
    clicked = (level > 0.0).astype(jnp.float32)
    weight = valid * (level - clicked) * scores
    if with_rhs:
        weight = valid * level - weight
    weight = weight.astype(jnp.bfloat16)
    terms = jnp.einsum("bul,bur->blr", weight.astype(jnp.float32), rows.astype(jnp.float32))
    return jax.ops.segment_sum(terms.reshape(-1, terms.shape[2]), lists.reshape(-1), num_segments=table.shape[0])


def user_part(users, confidence, item_lists, block_counts, requests, hot_table, cold_table, with_rhs):
    devices = N_WIDE * N_NARROW
    owners = jnp.arange(devices * CAP, dtype=jnp.int32) // CAP

    def advance(carry, index):
        hot_sum, cold_sum = carry
        wanted = owners * COLD_DEV + requests[index]
        table = jnp.concatenate([hot_table, cold_table[wanted]], 0)
        rows = lax.dynamic_slice_in_dim(users, index * (NB * UB), NB * UB, 0).reshape(NB, UB, R)
        level = lax.dynamic_slice_in_dim(confidence, index * NB, NB, 0)
        lists = lax.dynamic_slice_in_dim(item_lists, index * NB, NB, 0)
        counts = lax.dynamic_slice_in_dim(block_counts, index * NB, NB, 0)
        partial_value = block_terms(rows, level, lists, counts, table, with_rhs)
        return (hot_sum + partial_value[:HOT], cold_sum.at[wanted].add(partial_value[HOT:])), None

    start = (jnp.zeros((HOT, R), jnp.float32), jnp.zeros((COLD, R), jnp.float32))
    totals, unused = lax.scan(advance, start, jnp.arange(devices, dtype=jnp.int32))
    return [totals[0], totals[1]]


def apply_gram(direction, gram):
    return jnp.dot(direction, gram, precision=lax.Precision.HIGHEST) + REGULAR * direction


def reference(users, confidence, item_lists, block_counts, requests, hot_factors, cold_factors):
    gram = jnp.dot(users.T, users, preferred_element_type=jnp.float32)
    terms = user_part(users, confidence, item_lists, block_counts, requests,
                      hot_factors.astype(jnp.bfloat16), cold_factors.astype(jnp.bfloat16), True)
    solutions = [hot_factors, cold_factors]
    residuals = [terms[which] - apply_gram(solutions[which], gram) for which in range(2)]
    directions = list(residuals)
    norms = [jnp.sum(residual * residual, axis=1, keepdims=True) for residual in residuals]
    for step in range(ITERS):
        terms = user_part(users, confidence, item_lists, block_counts, requests,
                          directions[0].astype(jnp.bfloat16), directions[1].astype(jnp.bfloat16), False)
        for which in range(2):
            image = terms[which] + apply_gram(directions[which], gram)
            alpha = norms[which] / (jnp.sum(directions[which] * image, axis=1, keepdims=True) + EPS)
            solutions[which] = solutions[which] + alpha * directions[which]
            if step + 1 < ITERS:
                residuals[which] = residuals[which] - alpha * image
                fresh = jnp.sum(residuals[which] * residuals[which], axis=1, keepdims=True)
                directions[which] = residuals[which] + (fresh / (norms[which] + EPS)) * directions[which]
                norms[which] = fresh
    return solutions[0], solutions[1]
```

```python
import functools

import jax
import jax.numpy as jnp
from jax import lax
from jax.experimental import pallas as pl
from jax.experimental.pallas import tpu as pltpu
from jax.sharding import PartitionSpec as P

MESH = pl.DeviceIdType.MESH
REGULAR = 1.0
EPS = 1e-06
F32 = jnp.float32
BF = jnp.bfloat16
NDEV = 128
NCHIP = 64
RANK = 128
USERS = 2048
BLOCKS = 16
LENGTH = 512
HOT = 1024
HALF = 512
COLD = 512
TABLE = 1536
OWN = 8
CAP = 4
ROWS = 256
PIECE = 512
GROWS = 8
GOWNERS = 16


def dot(a, b):
    return jnp.dot(a, b, preferred_element_type=F32)


def halves(v):
    high = v.astype(BF)
    return high, (v - high.astype(F32)).astype(BF)


def turn(t):
    return 2 - t + 3 * (t // 2) - 2 * (t // 3)


def kernel(
    users, conf, lists, counts, reqs, hot, cold,
    hot_out, cold_out,
    users_t, stack, lmat, cmat, pick, place,
    send0, recv0, gpart, grecv, gram, gram2,
    csend, crecv,
    sib_out, sib_in, hsend, hrecv, hdir, scal,
    q_part, q_in, q_sum, q_recv,
    cold_sol, cold_res, cold_dir, ctable, cterm,
    sem0, gsem, csem, sibsem, hsem, fsem, qsem,
):
    w = lax.axis_index("wide")
    y = lax.axis_index("narrow")
    z = w // 8
    x = (w // 2) % 4
    k = w % 2
    me = w * 4 + y
    chip = (z * 4 + x) * 4 + y
    sibling = (w + 1 - 2 * k, y)

    def any_partner(t):
        z2 = (z + turn(t // 32)) % 4
        x2 = (x + turn((t // 8) % 4)) % 4
        y2 = (y + turn((t // 2) % 4)) % 4
        k2 = (k + 1 - t % 2) % 2
        w2 = (z2 * 4 + x2) * 2 + k2
        return (w2, y2), w2 * 4 + y2

    def core_partner(t):
        z2 = (z + turn(t // 16)) % 4
        x2 = (x + turn((t // 4) % 4)) % 4
        y2 = (y + turn(t % 4)) % 4
        return ((z2 * 4 + x2) * 2 + k, y2), (z2 * 4 + x2) * 4 + y2

    def loop(count, fn):
        def step(t, carry):
            fn(t)
            return carry

        lax.fori_loop(0, count, step, 0)

    def push(src, dst, send, recv, device):
        pltpu.make_async_remote_copy(
            src_ref=src, dst_ref=dst, send_sem=send, recv_sem=recv,
            device_id=device, device_id_type=MESH,
        ).start()

    def wait(ref, sem):
        pltpu.make_async_copy(ref, ref, sem).wait()

    barrier = pltpu.get_barrier_semaphore()

    def greet(t):
        device, _ = any_partner(t)
        pl.semaphore_signal(barrier, inc=1, device_id=device, device_id_type=MESH)

    loop(NDEV - 1, greet)

    for b in range(BLOCKS):
        users_t[:, b * 128:(b + 1) * 128] = users[b * 128:(b + 1) * 128, :].T
    gpart[...] = dot(users_t[...], users[...])
    owner_of = lax.broadcasted_iota(jnp.int32, (NDEV, COLD), 0)
    entry = lax.broadcasted_iota(jnp.int32, (NDEV, COLD), 1)
    mine = jnp.where((entry >> 2) == owner_of, reqs[...].astype(F32), 0.0)
    lanes_of = (
        (lax.broadcasted_iota(jnp.int32, (COLD, 128), 0) & 3)
        == lax.broadcasted_iota(jnp.int32, (COLD, 128), 1)
    )
    lane_pick = lanes_of.astype(F32).astype(BF)
    high, low = halves(mine)
    asked = dot(high, lane_pick) + dot(low, lane_pick)
    send0[...] = asked.reshape(NDEV, 1, 128)

    pl.semaphore_wait(barrier, NDEV - 1)

    def send_request(t):
        device, s2 = any_partner(t)
        push(send0.at[s2], recv0.at[me], sem0.at[0], sem0.at[1], device)

    loop(NDEV - 1, send_request)
    recv0[pl.ds(me, 1)] = send0[pl.ds(me, 1)]

    def send_gram(m):
        @pl.when(me != m * 8)
        def _():
            push(
                gpart.at[pl.ds(pl.multiple_of(m * GROWS, GROWS), GROWS)], grecv.at[me],
                gsem.at[0], gsem.at[1], (m * 2, 0),
            )

    loop(GOWNERS, send_gram)
    is_gram_owner = me % 8 == 0
    grow = pl.multiple_of((me // 8) * GROWS, GROWS)

    def build_block(b):
        turned = conf[b].T
        used = lax.broadcasted_iota(jnp.int32, (LENGTH, 128), 0) < counts[b]
        level = jnp.where(used, turned.astype(F32), 0.0)
        clicked = jnp.where(level > 0.0, 1.0, 0.0)
        stack[:, :128] = level.astype(BF)
        stack[:, 128:] = clicked.astype(BF)
        listed = lists[pl.ds(b, 1), :]
        column = pl.ds(pl.multiple_of(b * 128, 128), 128)

        def build_rows(i):
            base = pl.multiple_of(i * ROWS, ROWS)
            row = lax.broadcasted_iota(jnp.int32, (ROWS, LENGTH), 0) + base
            chosen = jnp.where(row == listed, 1.0, 0.0).astype(BF)
            both = dot(chosen, stack[...])
            level_sum = both[:, :128]
            lmat[pl.ds(base, ROWS), column] = level_sum.astype(BF)
            cmat[pl.ds(base, ROWS), column] = (level_sum - both[:, 128:]).astype(BF)

        loop(TABLE // ROWS, build_rows)

    loop(BLOCKS // 2, build_block)

    wait(recv0.at[pl.ds(0, NDEV - 1)], sem0.at[1])
    wanted = recv0[...].reshape(NDEV, 128)
    spread = (
        (lax.broadcasted_iota(jnp.int32, (COLD, NDEV), 0) >> 2)
        == lax.broadcasted_iota(jnp.int32, (COLD, NDEV), 1)
    ).astype(F32).astype(BF)
    high, low = halves(wanted)
    rows4 = jnp.where(lanes_of, dot(spread, high) + dot(spread, low), 0.0)
    wanted_col = jnp.sum(rows4, axis=1, keepdims=True).astype(jnp.int32)
    wanted_wide = jnp.broadcast_to(wanted_col, (COLD, 128))
    wanted_row = wanted_wide.astype(F32).T[0:1, :].astype(jnp.int32)
    lane_item = lax.broadcasted_iota(jnp.int32, (COLD, COLD), 1)
    row_item = lax.broadcasted_iota(jnp.int32, (COLD, COLD), 0)
    pick[...] = jnp.where(wanted_col == lane_item, 1.0, 0.0).astype(BF)
    place[...] = jnp.where(wanted_row == row_item, 1.0, 0.0).astype(BF)

    def cold_exchange(e, rows):
        csend[e] = rows.reshape(NDEV, CAP, 128)

        def go(t):
            device, s2 = any_partner(t)
            push(csend.at[e, s2], crecv.at[e, me], csem.at[e, 0], csem.at[e, 1], device)

        loop(NDEV - 1, go)
        crecv[e, pl.ds(me, 1)] = csend[e, pl.ds(me, 1)]

    def cold_arrived(e):
        wait(crecv.at[e, pl.ds(0, NDEV - 1)], csem.at[e, 1])
        return crecv[e].reshape(COLD, 128)

    def cold_fetch(e, values):
        cold_exchange(e, dot(pick[...], values.astype(BF)))

    def cold_placed(e):
        high, low = halves(cold_arrived(e))
        return dot(place[...], high) + dot(place[...], low)

    cold_sol[...] = cold[...]
    cold_fetch(0, cold[...])

    @pl.when(is_gram_owner)
    def _():
        wait(grecv.at[pl.ds(0, NDEV - 1)], gsem.at[1])
        grecv[pl.ds(me, 1)] = gpart[pl.ds(grow, GROWS), :].reshape(1, GROWS, 128)
        gram[pl.ds(grow, GROWS), :] = jnp.sum(grecv[...], axis=0)

        def go(t):
            device, _ = any_partner(t)
            push(
                gram.at[pl.ds(grow, GROWS)], gram.at[pl.ds(grow, GROWS)],
                gsem.at[2], gsem.at[3], device,
            )

        loop(NDEV - 1, go)

    def second_half(b):
        build_block(b + BLOCKS // 2)

    loop(BLOCKS // 2, second_half)

    def user_terms(table, base, opening):
        total = jnp.zeros((ROWS, RANK), F32)
        for at in range(0, USERS, PIECE):
            scores = dot(table, users_t[:, at:at + PIECE])
            weight = cmat[pl.ds(base, ROWS), at:at + PIECE].astype(F32) * scores
            if opening:
                weight = lmat[pl.ds(base, ROWS), at:at + PIECE].astype(F32) - weight
            total = total + dot(weight.astype(BF), users[at:at + PIECE, :])
        return total

    def user_squares(table, base):
        total = jnp.zeros((ROWS, 128), F32)
        for at in range(0, USERS, PIECE):
            scores = dot(table, users_t[:, at:at + PIECE])
            part = cmat[pl.ds(base, ROWS), at:at + PIECE].astype(F32) * scores * scores
            for lane in range(0, PIECE, 128):
                total = total + part[:, lane:lane + 128]
        return total

    other_base = (1 - k) * HALF
    own_base = k * HALF

    def hot_give(g, read_table, opening):
        def for_sibling(i):
            local = pl.multiple_of(i * ROWS, ROWS)
            base = pl.multiple_of(other_base + i * ROWS, ROWS)
            rows = pl.ds(local, ROWS)
            sib_out[g, rows, :] = user_terms(read_table(base), base, opening)
            push(
                sib_out.at[g, rows], sib_in.at[g, rows],
                sibsem.at[g, 0], sibsem.at[g, 1], sibling,
            )

        loop(HALF // ROWS, for_sibling)

        def for_own(i):
            local = pl.multiple_of(i * ROWS, ROWS)
            base = pl.multiple_of(own_base + i * ROWS, ROWS)
            hsend[g, pl.ds(local, ROWS), :] = user_terms(read_table(base), base, opening)

        loop(HALF // ROWS, for_own)
        wait(sib_in.at[g], sibsem.at[g, 1])
        hsend[g] = hsend[g] + sib_in[g]

        def go(t):
            device, c2 = core_partner(t)
            push(
                hsend.at[g, pl.ds(pl.multiple_of(c2 * OWN, OWN), OWN)], hrecv.at[g, chip],
                hsem.at[g, 0], hsem.at[g, 1], device,
            )

        loop(NCHIP - 1, go)
        hrecv[g, pl.ds(chip, 1)] = hsend[
            g, pl.ds(pl.multiple_of(chip * OWN, OWN), OWN), :
        ].reshape(1, OWN, 128)

    def hot_given(g):
        wait(hrecv.at[g, pl.ds(0, NCHIP - 1)], hsem.at[g, 1])
        return jnp.sum(hrecv[g], axis=0)

    own_rows = pl.ds(pl.multiple_of(own_base + chip * OWN, OWN), OWN)
    own_half = pl.ds(pl.multiple_of(own_base, HALF), HALF)

    def hot_spread(buf, f, values):
        buf[own_rows, :] = values

        def go(t):
            device, _ = core_partner(t)
            push(buf.at[own_rows], buf.at[own_rows], fsem.at[f, 0], fsem.at[f, 1], device)

        loop(NCHIP - 1, go)

    def hot_forward(buf, f):
        wait(buf.at[pl.ds(0, (NCHIP - 1) * OWN)], fsem.at[f, 1])
        push(buf.at[own_half], buf.at[own_half], fsem.at[f, 2], fsem.at[f, 3], sibling)

    def hot_forwarded(buf, f):
        wait(buf.at[pl.ds(0, HALF)], fsem.at[f, 3])

    def read_rows(buf):
        return lambda base: buf[pl.ds(base, ROWS), :].astype(BF)

    def cold_give(e, table, opening):
        ctable[...] = table.astype(BF)

        def rows(i):
            local = pl.ds(pl.multiple_of(i * ROWS, ROWS), ROWS)
            base = pl.multiple_of(HOT + i * ROWS, ROWS)
            cterm[local, :] = user_terms(ctable[local, :], base, opening)

        loop(COLD // ROWS, rows)
        cold_exchange(e, cterm[...])

    def apply_gram(v):
        high, low = halves(v)
        return dot(high, gram2[0]) + dot(high, gram2[1]) + dot(low, gram2[0]) + REGULAR * v

    def row_sum(v):
        return jnp.sum(v, axis=1, keepdims=True)

    hot_give(0, read_rows(hot), True)
    cold_give(1, cold_arrived(0), True)

    @pl.when(is_gram_owner)
    def _():
        wait(gram.at[pl.ds(0, (GOWNERS - 1) * GROWS)], gsem.at[3])

    @pl.when(jnp.logical_not(is_gram_owner))
    def _():
        wait(gram, gsem.at[3])

    gram2[0], gram2[1] = halves(gram[...])
    hot_res = hot_given(0) - apply_gram(hot[own_rows, :])
    hot_dir = hot_res
    hot_norm = row_sum(hot_res * hot_res)
    hdir0 = hdir.at[0]
    hdir1 = hdir.at[1]
    hot_spread(hdir0, 0, hot_dir)

    cold_res[...] = cold_placed(1) - apply_gram(cold_sol[...])
    cold_fetch(2, cold_res[...])
    cold_norm = row_sum(cold_res[...] * cold_res[...])

    hot_forward(hdir0, 0)
    hot_forwarded(hdir0, 0)
    hot_give(1, read_rows(hdir0), False)
    cold_give(3, cold_arrived(2), False)

    image = hot_given(1) + apply_gram(hot_dir)
    hot_alpha = hot_norm / (row_sum(hot_dir * image) + EPS)
    hot_res = hot_res - hot_alpha * image
    fresh = row_sum(hot_res * hot_res)
    hot_dir = hot_res + fresh / (hot_norm + EPS) * hot_dir
    hot_spread(hdir1, 1, hot_dir)
    curve = row_sum(hot_dir * apply_gram(hot_dir))
    lane = lax.broadcasted_iota(jnp.int32, (OWN, 128), 1)
    hot_spread(
        scal, 2,
        jnp.where(lane < 32, hot_alpha, jnp.where(lane < 64, fresh, curve)),
    )

    image = cold_placed(3) + apply_gram(cold_res[...])
    cold_alpha = cold_norm / (row_sum(cold_res[...] * image) + EPS)
    cold_sol[...] = cold_sol[...] + cold_alpha * cold_res[...]
    residual = cold_res[...] - cold_alpha * image
    fresh = row_sum(residual * residual)
    cold_dir[...] = residual + fresh / (cold_norm + EPS) * cold_res[...]
    cold_norm = fresh
    cold_fetch(4, cold_dir[...])
    cold_curve = row_sum(cold_dir[...] * apply_gram(cold_dir[...]))

    hot_forward(hdir1, 1)
    hot_forwarded(hdir1, 1)
    hot_forward(scal, 2)
    def hot_squares(i):
        rows = pl.ds(pl.multiple_of(i * ROWS, ROWS), ROWS)
        square = user_squares(hdir[1, rows, :].astype(BF), pl.multiple_of(i * ROWS, ROWS))
        for j in range(ROWS // 128):
            q_part[pl.ds(i * (ROWS // 128) + j, 1), :] = jnp.sum(
                square[j * 128:(j + 1) * 128, :].T, axis=0, keepdims=True
            )

    loop(HOT // ROWS, hot_squares)
    push(q_part, q_in, qsem.at[0], qsem.at[1], sibling)
    wait(q_in, qsem.at[1])
    q_sum[...] = q_part[...] + q_in[...]

    def send_q(t):
        device, _ = core_partner(t)
        push(q_sum, q_recv.at[chip], qsem.at[2], qsem.at[3], device)

    loop(NCHIP - 1, send_q)
    q_recv[pl.ds(chip, 1)] = q_sum[...].reshape(1, OWN, 128)

    ctable[...] = cold_arrived(4).astype(BF)

    def cold_squares(i):
        local = pl.ds(pl.multiple_of(i * ROWS, ROWS), ROWS)
        base = pl.multiple_of(HOT + i * ROWS, ROWS)
        cterm[local, :] = user_squares(ctable[local, :], base)

    loop(COLD // ROWS, cold_squares)
    cold_exchange(5, cterm[...])

    hot_forwarded(scal, 2)
    wait(q_recv.at[pl.ds(0, NCHIP - 1)], qsem.at[3])
    q_all = jnp.sum(q_recv[...], axis=0)
    q_col = q_all.T
    for a in range(HOT // 128):
        rows = slice(a * 128, (a + 1) * 128)
        alpha = scal[rows, 32:33] / (q_col[:, a:a + 1] + scal[rows, 64:65] + EPS)
        hot_out[rows, :] = (
            hot[rows, :] + scal[rows, 0:1] * hdir[0, rows, :] + alpha * hdir[1, rows, :]
        )

    square = row_sum(cold_placed(5))
    alpha = cold_norm / (square + cold_curve + EPS)
    cold_out[...] = cold_sol[...] + alpha * cold_dir[...]

    wait(send0.at[pl.ds(0, NDEV - 1)], sem0.at[0])

    @pl.when(is_gram_owner)
    def _():
        wait(grecv.at[pl.ds(0, GOWNERS - 1)], gsem.at[0])
        wait(grecv.at[pl.ds(0, NDEV - 1)], gsem.at[2])

    @pl.when(jnp.logical_not(is_gram_owner))
    def _():
        wait(grecv.at[pl.ds(0, GOWNERS)], gsem.at[0])

    for e in range(6):
        wait(csend.at[e, pl.ds(0, NDEV - 1)], csem.at[e, 0])
    for g in range(2):
        wait(sib_out.at[g], sibsem.at[g, 0])
        wait(hrecv.at[g, pl.ds(0, NCHIP - 1)], hsem.at[g, 0])
    for f in range(3):
        wait(hrecv.at[0, pl.ds(0, NCHIP - 1)], fsem.at[f, 0])
        wait(scal.at[pl.ds(0, HALF)], fsem.at[f, 2])
    wait(q_part, qsem.at[0])
    wait(q_recv.at[pl.ds(0, NCHIP - 1)], qsem.at[2])


def body(users, confidence, item_lists, block_counts, requests, hot_factors, cold_factors):
    vmem = pl.BlockSpec(memory_space=pltpu.VMEM)
    smem = pl.BlockSpec(memory_space=pltpu.SMEM)
    dma = pltpu.SemaphoreType.DMA
    return pl.pallas_call(
        kernel,
        out_shape=(
            jax.ShapeDtypeStruct((HOT, RANK), F32),
            jax.ShapeDtypeStruct((COLD, RANK), F32),
        ),
        in_specs=[vmem, vmem, vmem, smem, vmem, vmem, vmem],
        out_specs=(vmem, vmem),
        scratch_shapes=[
            pltpu.VMEM((RANK, USERS), BF),
            pltpu.VMEM((LENGTH, 256), BF),
            pltpu.VMEM((TABLE, USERS), BF),
            pltpu.VMEM((TABLE, USERS), BF),
            pltpu.VMEM((COLD, COLD), BF),
            pltpu.VMEM((COLD, COLD), BF),
            pltpu.VMEM((NDEV, 1, 128), F32),
            pltpu.VMEM((NDEV, 1, 128), F32),
            pltpu.VMEM((RANK, RANK), F32),
            pltpu.VMEM((NDEV, GROWS, 128), F32),
            pltpu.VMEM((RANK, RANK), F32),
            pltpu.VMEM((2, RANK, RANK), BF),
            pltpu.VMEM((6, NDEV, CAP, 128), F32),
            pltpu.VMEM((6, NDEV, CAP, 128), F32),
            pltpu.VMEM((2, HALF, 128), F32),
            pltpu.VMEM((2, HALF, 128), F32),
            pltpu.VMEM((2, HALF, 128), F32),
            pltpu.VMEM((2, NCHIP, OWN, 128), F32),
            pltpu.VMEM((2, HOT, 128), F32),
            pltpu.VMEM((HOT, 128), F32),
            pltpu.VMEM((OWN, 128), F32),
            pltpu.VMEM((OWN, 128), F32),
            pltpu.VMEM((OWN, 128), F32),
            pltpu.VMEM((NCHIP, OWN, 128), F32),
            pltpu.VMEM((COLD, RANK), F32),
            pltpu.VMEM((COLD, RANK), F32),
            pltpu.VMEM((COLD, RANK), F32),
            pltpu.VMEM((COLD, RANK), BF),
            pltpu.VMEM((COLD, RANK), F32),
            dma((2,)),
            dma((4,)),
            dma((6, 2)),
            dma((2, 2)),
            dma((2, 2)),
            dma((3, 4)),
            dma((4,)),
        ],
        compiler_params=pltpu.CompilerParams(
            collective_id=0, has_side_effects=True, vmem_limit_bytes=56 << 20
        ),
    )(users, confidence, item_lists, block_counts, requests, hot_factors, cold_factors)


def solution(mesh):
    both = ("wide", "narrow")
    placed = (
        P(both, None),
        P(both, None, None),
        P(both, None),
        P(both),
        P(both, None),
        P(),
        P(both, None),
    )
    return jax.shard_map(
        body,
        mesh=mesh,
        in_specs=placed,
        out_specs=(P(), P(both, None)),
        check_vma=False,
    )
```

```python
import functools

import jax
import jax.numpy as jnp
from jax import lax
from jax.experimental import pallas as pl
from jax.experimental.pallas import tpu as pltpu
from jax.sharding import PartitionSpec as P

MESH = pl.DeviceIdType.MESH
REGULAR = 1.0
EPS = 1e-06
F32 = jnp.float32
BF = jnp.bfloat16
NDEV = 128
NCHIP = 64
RANK = 128
USERS = 2048
BLOCKS = 16
LENGTH = 512
HOT = 1024
HALF = 512
COLD = 512
TABLE = 1536
OWN = 8
CAP = 4
ROWS = 256
PIECE = 512
EARLY = 6


def dot(a, b):
    return jnp.dot(a, b, preferred_element_type=F32)


def halves(v):
    high = v.astype(BF)
    return high, (v - high.astype(F32)).astype(BF)


def turn(a):
    return 2 - a + 3 * (a // 2) - 2 * ((a + 1) // 4)


def kernel(
    users_in, conf_in, lists_in, counts_in, reqs_in, hot_in, cold_in,
    hot_out, cold_out,
    users, conf, lists, counts, reqs, hot, cold, hot_sol, users_t, stack, lmat, cmat, pick, place,
    send0, recv0, first_send, first_recv, gram2,
    csend, crecv,
    sib_out, sib_in, hsend, hrecv, hdir, scal,
    q_part, q_in, q_sum, q_recv,
    cold_sol, cold_res, cold_dir, cold_image,
    insem, sem0, csem, sibsem, hsem, fsem, qsem,
):
    w = lax.axis_index("wide")
    y = lax.axis_index("narrow")
    z = w // 8
    x = (w // 2) % 4
    k = w % 2
    me = w * 4 + y
    chip = (z * 4 + x) * 4 + y
    sibling = (w + 1 - 2 * k, y)

    ys = [lax.rem(y + d, 4) for d in (2, 1, 3, 0)]

    def each_chip(fn):
        def planes(a, carry):
            z2 = lax.rem(z + turn(a), 4)

            def rows(b, inner):
                zx = z2 * 4 + lax.rem(x + turn(b), 4)
                here = jnp.logical_and(a == 3, b == 3)
                for place_at, y2 in enumerate(ys):
                    fn(zx, y2, here if place_at == 3 else None)
                return inner

            return lax.fori_loop(0, 4, rows, carry)

        lax.fori_loop(0, 4, planes, 0)

    def each_other(fn):
        def both_cores(zx, y2, here):
            for core in (1 - k, k):
                w2 = zx * 2 + core
                if here is None or core is not k:
                    fn((w2, y2), w2 * 4 + y2)
                else:
                    pl.when(jnp.logical_not(here))(lambda: fn((w2, y2), w2 * 4 + y2))

        each_chip(both_cores)

    def each_same_core(fn):
        def one(zx, y2, here):
            if here is None:
                fn((zx * 2 + k, y2), zx * 4 + y2)
            else:
                pl.when(jnp.logical_not(here))(lambda: fn((zx * 2 + k, y2), zx * 4 + y2))

        each_chip(one)

    def loop(count, fn, unroll=1):
        def step(t, carry):
            fn(t)
            return carry

        lax.fori_loop(0, count, step, 0, unroll=unroll)

    def push(src, dst, send, recv, device):
        pltpu.make_async_remote_copy(
            src_ref=src, dst_ref=dst, send_sem=send, recv_sem=recv,
            device_id=device, device_id_type=MESH,
        ).start()

    def wait(ref, sem):
        pltpu.make_async_copy(ref, ref, sem).wait()

    loads = [
        pltpu.make_async_copy(src, dst, insem.at[i])
        for i, (src, dst) in enumerate(
            (
                (users_in, users), (conf_in, conf), (hot_in, hot), (cold_in, cold),
                (reqs_in, reqs), (lists_in, lists), (counts_in, counts),
            )
        )
    ]
    for load in loads:
        load.start()
    barrier = pltpu.get_barrier_semaphore()

    def greet(device, _):
        pl.semaphore_signal(barrier, inc=1, device_id=device, device_id_type=MESH)

    each_other(greet)

    loads[4].wait()
    owner_of = lax.broadcasted_iota(jnp.int32, (NDEV, COLD), 0)
    entry = lax.broadcasted_iota(jnp.int32, (NDEV, COLD), 1)
    mine = jnp.where((entry >> 2) == owner_of, reqs[...].astype(F32), 0.0)
    lanes_of = (
        (lax.broadcasted_iota(jnp.int32, (COLD, 128), 0) & 3)
        == lax.broadcasted_iota(jnp.int32, (COLD, 128), 1)
    )
    lane_pick = lanes_of.astype(F32).astype(BF)
    high, low = halves(mine)
    asked = dot(high, lane_pick) + dot(low, lane_pick)
    send0[:, 0:1, :] = asked.reshape(NDEV, 1, 128)
    loads[0].wait()
    for b in range(BLOCKS):
        users_t[:, b * 128:(b + 1) * 128] = users[b * 128:(b + 1) * 128, :].T
    send0[:, 1:2, :] = dot(users_t[...], users[...]).reshape(NDEV, 1, 128)
    loads[1].wait()
    loads[5].wait()
    loads[6].wait()

    def fold(b, first, last, shift):
        listed = lists[pl.ds(b, 1), :]
        column = pl.ds(pl.multiple_of(b * 128, 128), 128)
        row = lax.broadcasted_iota(jnp.int32, (ROWS, LENGTH), 0).astype(F32).astype(BF)
        for base in range(first, last, ROWS):
            near = jnp.clip(listed - base, -1, ROWS).astype(F32).astype(BF)
            chosen = jnp.where(row == near, jnp.ones((), BF), jnp.zeros((), BF))
            both = dot(chosen, stack[b])
            level_sum = both[:, :128]
            lmat[base:base + ROWS, column] = level_sum.astype(BF)
            cmat[base:base + ROWS, column] = (level_sum - both[:, 128:] + shift).astype(BF)

    def fold_hot(b):
        used = lax.broadcasted_iota(jnp.int32, (LENGTH, 128), 0) < counts[b]
        level = jnp.where(used, conf[b].T.astype(F32), 0.0)
        clicked = jnp.where(level > 0.0, 1.0, 0.0)
        stack[b, :, :128] = level.astype(BF)
        stack[b, :, 128:] = clicked.astype(BF)
        fold(b, 0, HOT, 1.0)

    def fold_cold(b):
        fold(b, HOT, TABLE, 0.0)

    loop(EARLY, fold_hot)
    pl.semaphore_wait(barrier, NDEV - 1)

    def send_request(device, s2):
        push(send0.at[s2], recv0.at[me], sem0.at[0], sem0.at[1], device)

    each_other(send_request)
    recv0[pl.ds(me, 1)] = send0[pl.ds(me, 1)]

    def fold_late(b):
        fold_hot(b + EARLY)

    loop(BLOCKS - EARLY, fold_late)

    def cold_exchange(e, rows):
        csend[e] = rows.reshape(NDEV, CAP, 128)

        def go(device, s2):
            push(csend.at[e, s2], crecv.at[e, me], csem.at[e, 0], csem.at[e, 1], device)

        each_other(go)
        crecv[e, pl.ds(me, 1)] = csend[e, pl.ds(me, 1)]

    def cold_arrived(e):
        wait(crecv.at[e, pl.ds(0, NDEV - 1)], csem.at[e, 1])
        return crecv[e].reshape(COLD, 128)

    def cold_fetch(e, values):
        cold_exchange(e, dot(pick[...], values.astype(BF)))

    def cold_placed(e):
        high, low = halves(cold_arrived(e))
        both = dot(place[...], jnp.concatenate([high, low], axis=1))
        return both[:, :128] + both[:, 128:]

    def user_terms(table, base, opening):
        rows = pl.ds(base, HALF)
        total = jnp.zeros((HALF, RANK), F32)
        for at in range(0, USERS, PIECE):
            scores = dot(table, users_t[:, at:at + PIECE])
            weight = cmat[rows, at:at + PIECE].astype(F32) * scores
            if opening:
                weight = lmat[rows, at:at + PIECE].astype(F32) - weight
            total = total + dot(weight.astype(BF), users[at:at + PIECE, :])
        return total

    def user_squares(table, base):
        rows = pl.ds(base, HALF)
        total = jnp.zeros((HALF, 128), F32)
        for at in range(0, USERS, PIECE):
            scores = dot(table, users_t[:, at:at + PIECE])
            part = cmat[rows, at:at + PIECE].astype(F32) * scores * scores
            for lane in range(0, PIECE, 128):
                total = total + part[:, lane:lane + 128]
        return total

    other_base = (1 - k) * HALF
    own_base = k * HALF

    def hot_give_sibling(g, read_table, opening):
        base = pl.multiple_of(other_base, HALF)
        sib_out[g] = user_terms(read_table(base), base, opening)
        push(sib_out.at[g], sib_in.at[g], sibsem.at[g, 0], sibsem.at[g, 1], sibling)

    def hot_give_own(g, read_table, opening):
        base = pl.multiple_of(own_base, HALF)
        own = user_terms(read_table(base), base, opening)
        wait(sib_in.at[g], sibsem.at[g, 1])
        hsend[g] = own + sib_in[g]

        def go(device, c2):
            push(
                hsend.at[g, pl.ds(pl.multiple_of(c2 * OWN, OWN), OWN)], hrecv.at[g, chip],
                hsem.at[g, 0], hsem.at[g, 1], device,
            )

        each_same_core(go)
        hrecv[g, pl.ds(chip, 1)] = hsend[
            g, pl.ds(pl.multiple_of(chip * OWN, OWN), OWN), :
        ].reshape(1, OWN, 128)

    def hot_given(g):
        wait(hrecv.at[g, pl.ds(0, NCHIP - 1)], hsem.at[g, 1])
        return jnp.sum(hrecv[g], axis=0)

    own_rows = pl.ds(pl.multiple_of(own_base + chip * OWN, OWN), OWN)
    own_half = pl.ds(pl.multiple_of(own_base, HALF), HALF)

    def hot_spread(buf, f, values):
        buf[own_rows, :] = values

        def go(device, _):
            push(buf.at[own_rows], buf.at[own_rows], fsem.at[f, 0], fsem.at[f, 1], device)

        each_same_core(go)

    def hot_forward(buf, f):
        wait(buf.at[pl.ds(0, (NCHIP - 1) * OWN)], fsem.at[f, 1])
        push(buf.at[own_half], buf.at[own_half], fsem.at[f, 2], fsem.at[f, 3], sibling)

    def hot_forwarded(buf, f):
        wait(buf.at[pl.ds(0, HALF)], fsem.at[f, 3])

    def read_rows(buf):
        return lambda base: buf[pl.ds(base, HALF), :].astype(BF)

    def cold_give(e, table, opening):
        cold_exchange(e, user_terms(table.astype(BF), HOT, opening))

    def apply_gram(v):
        high, low = halves(v)
        return dot(high, gram2[0]) + dot(high, gram2[1]) + dot(low, gram2[0]) + REGULAR * v

    def row_sum(v):
        return jnp.sum(v, axis=1, keepdims=True)

    loads[2].wait()
    hot_give_sibling(0, read_rows(hot), True)

    wait(recv0.at[pl.ds(0, NDEV - 1)], sem0.at[1])
    high, low = halves(recv0[:, 0:1, :].reshape(NDEV, 128))
    spread = (
        (lax.broadcasted_iota(jnp.int32, (COLD, NDEV), 0) >> 2)
        == lax.broadcasted_iota(jnp.int32, (COLD, NDEV), 1)
    ).astype(F32).astype(BF)
    rows4 = jnp.where(lanes_of, dot(spread, high) + dot(spread, low), 0.0)
    wanted_col = row_sum(rows4).astype(jnp.int32)
    lane_item = lax.broadcasted_iota(jnp.int32, (COLD, COLD), 1)
    pick[...] = jnp.where(wanted_col == lane_item, 1.0, 0.0).astype(BF)
    loads[3].wait()
    first_send[:, 0:CAP, :] = dot(pick[...], cold[...].astype(BF)).reshape(NDEV, CAP, 128)
    gram_row = jnp.sum(recv0[:, 1:2, :], axis=0, keepdims=True)
    first_send[:, CAP:, :] = jnp.broadcast_to(gram_row, (NDEV, 1, 128))

    def send_first(device, s2):
        push(first_send.at[s2], first_recv.at[me], csem.at[0, 0], csem.at[0, 1], device)

    each_other(send_first)
    first_recv[pl.ds(me, 1)] = first_send[pl.ds(me, 1)]
    wanted_wide = jnp.broadcast_to(wanted_col, (COLD, 128))
    wanted_row = wanted_wide.astype(F32).T[0:1, :].astype(jnp.int32)
    row_item = lax.broadcasted_iota(jnp.int32, (COLD, COLD), 0)
    place[...] = jnp.where(wanted_row == row_item, 1.0, 0.0).astype(BF)

    hot_give_own(0, read_rows(hot), True)
    loop(BLOCKS, fold_cold, unroll=4)

    wait(first_recv.at[pl.ds(0, NDEV - 1)], csem.at[0, 1])
    cold_give(1, first_recv[:, 0:CAP, :].reshape(COLD, 128), True)

    hot_res = hot_given(0) - REGULAR * hot[own_rows, :]
    hot_dir = hot_res
    hot_norm = row_sum(hot_res * hot_res)
    hdir0 = hdir.at[0]
    hdir1 = hdir.at[1]
    hot_spread(hdir0, 0, hot_dir)

    gram2[0], gram2[1] = halves(first_recv[:, CAP:, :].reshape(RANK, RANK))
    cold_image[...] = apply_gram(cold[...])
    residual = cold_placed(1) - cold_image[...]
    cold_res[...] = residual
    cold_fetch(2, residual)
    cold_norm = row_sum(residual * residual)
    cold_image[...] = apply_gram(residual)
    cold_curve = row_sum(residual * cold_image[...])

    hot_forward(hdir0, 0)
    hot_forwarded(hdir0, 0)
    hot_give_sibling(1, read_rows(hdir0), False)
    hot_give_own(1, read_rows(hdir0), False)
    cold_give(3, cold_arrived(2), False)

    image = hot_given(1) + REGULAR * hot_dir
    hot_alpha = hot_norm / (row_sum(hot_dir * image) + EPS)
    hot_res = hot_res - hot_alpha * image
    fresh = row_sum(hot_res * hot_res)
    hot_dir = hot_res + fresh / (hot_norm + EPS) * hot_dir
    hot_spread(hdir1, 1, hot_dir)
    lane = lax.broadcasted_iota(jnp.int32, (OWN, 128), 1)
    scal_own = jnp.where(lane < 64, hot_alpha, fresh)

    term = cold_placed(3)
    old = cold_res[...]
    cold_alpha = cold_norm / (row_sum(old * term) + cold_curve + EPS)
    residual = old - cold_alpha * (term + cold_image[...])
    fresh = row_sum(residual * residual)
    direction = residual + fresh / (cold_norm + EPS) * old
    cold_fetch(4, direction)
    cold_sol[...] = cold[...] + cold_alpha * old
    cold_dir[...] = direction
    cold_norm = fresh
    cold_curve = row_sum(direction * apply_gram(direction))
    hot_spread(scal, 2, scal_own)

    hot_forward(hdir1, 1)

    def hot_squares(base):
        start = pl.multiple_of(base, HALF)
        square = user_squares(hdir[1, pl.ds(start, HALF), :].astype(BF), start)
        for j in range(HALF // 128):
            q_part[pl.ds(start // 128 + j, 1), :] = jnp.sum(
                square[j * 128:(j + 1) * 128, :].T, axis=0, keepdims=True
            )

    hot_squares(own_base)
    hot_forwarded(hdir1, 1)
    hot_squares(other_base)
    push(q_part, q_in, qsem.at[0], qsem.at[1], sibling)
    wait(q_in, qsem.at[1])
    q_sum[...] = q_part[...] + q_in[...]

    def send_q(device, _):
        push(q_sum, q_recv.at[chip], qsem.at[2], qsem.at[3], device)

    each_same_core(send_q)
    q_recv[pl.ds(chip, 1)] = q_sum[...].reshape(1, OWN, 128)

    cold_exchange(5, user_squares(cold_arrived(4).astype(BF), HOT))

    hot_forward(scal, 2)
    hot_forwarded(scal, 2)
    curves = []
    for a in range(HOT // 128):
        rows = slice(a * 128, (a + 1) * 128)
        d1 = hdir[1, rows, :]
        curves.append(REGULAR * row_sum(d1 * d1) + EPS)
        hot_sol[rows, :] = hot[rows, :] + scal[rows, 0:1] * hdir[0, rows, :]
    wait(q_recv.at[pl.ds(0, NCHIP - 1)], qsem.at[3])
    q_col = jnp.sum(q_recv[...], axis=0).T
    for a in range(HOT // 128):
        rows = slice(a * 128, (a + 1) * 128)
        alpha = scal[rows, 64:65] / (q_col[:, a:a + 1] + curves[a])
        hot_sol[rows, :] = hot_sol[rows, :] + alpha * hdir[1, rows, :]
    hot_store = pltpu.make_async_copy(hot_sol, hot_out, insem.at[7])
    hot_store.start()

    alpha = cold_norm / (row_sum(cold_placed(5)) + cold_curve + EPS)
    cold_sol[...] = cold_sol[...] + alpha * cold_dir[...]
    cold_store = pltpu.make_async_copy(cold_sol, cold_out, insem.at[8])
    cold_store.start()

    wait(send0.at[pl.ds(0, NDEV - 1)], sem0.at[0])

    wait(first_send.at[pl.ds(0, NDEV - 1)], csem.at[0, 0])
    for e in range(1, 6):
        wait(csend.at[e, pl.ds(0, NDEV - 1)], csem.at[e, 0])
    for g in range(2):
        wait(sib_out.at[g], sibsem.at[g, 0])
        wait(hrecv.at[g, pl.ds(0, NCHIP - 1)], hsem.at[g, 0])
    for f in range(3):
        wait(hrecv.at[0, pl.ds(0, NCHIP - 1)], fsem.at[f, 0])
        wait(scal.at[pl.ds(0, HALF)], fsem.at[f, 2])
    wait(q_part, qsem.at[0])
    wait(q_recv.at[pl.ds(0, NCHIP - 1)], qsem.at[2])
    hot_store.wait()
    cold_store.wait()


def hand_over(hot_in, cold_in, hot_out, cold_out):
    hot_out[...] = hot_in[...]
    cold_out[...] = cold_in[...]


def body(users, confidence, item_lists, block_counts, requests, hot_factors, cold_factors):
    hbm = pl.BlockSpec(memory_space=pl.ANY)
    dma = pltpu.SemaphoreType.DMA
    outs = (
        jax.ShapeDtypeStruct((HOT, RANK), F32),
        jax.ShapeDtypeStruct((COLD, RANK), F32),
    )
    results = pl.pallas_call(
        kernel,
        out_shape=outs,
        in_specs=[hbm] * 7,
        out_specs=(hbm, hbm),
        scratch_shapes=[
            pltpu.VMEM((USERS, RANK), BF),
            pltpu.VMEM((BLOCKS, 128, LENGTH), BF),
            pltpu.VMEM((BLOCKS, LENGTH), jnp.int32),
            pltpu.SMEM((BLOCKS,), jnp.int32),
            pltpu.VMEM((1, COLD), jnp.int32),
            pltpu.VMEM((HOT, RANK), F32),
            pltpu.VMEM((COLD, RANK), F32),
            pltpu.VMEM((HOT, RANK), F32),
            pltpu.VMEM((RANK, USERS), BF),
            pltpu.VMEM((BLOCKS, LENGTH, 256), BF),
            pltpu.VMEM((TABLE, USERS), BF),
            pltpu.VMEM((TABLE, USERS), BF),
            pltpu.VMEM((COLD, COLD), BF),
            pltpu.VMEM((COLD, COLD), BF),
            pltpu.VMEM((NDEV, 2, 128), F32),
            pltpu.VMEM((NDEV, 2, 128), F32),
            pltpu.VMEM((NDEV, CAP + 1, 128), F32),
            pltpu.VMEM((NDEV, CAP + 1, 128), F32),
            pltpu.VMEM((2, RANK, RANK), BF),
            pltpu.VMEM((6, NDEV, CAP, 128), F32),
            pltpu.VMEM((6, NDEV, CAP, 128), F32),
            pltpu.VMEM((2, HALF, 128), F32),
            pltpu.VMEM((2, HALF, 128), F32),
            pltpu.VMEM((2, HALF, 128), F32),
            pltpu.VMEM((2, NCHIP, OWN, 128), F32),
            pltpu.VMEM((2, HOT, 128), F32),
            pltpu.VMEM((HOT, 128), F32),
            pltpu.VMEM((OWN, 128), F32),
            pltpu.VMEM((OWN, 128), F32),
            pltpu.VMEM((OWN, 128), F32),
            pltpu.VMEM((NCHIP, OWN, 128), F32),
            pltpu.VMEM((COLD, RANK), F32),
            pltpu.VMEM((COLD, RANK), F32),
            pltpu.VMEM((COLD, RANK), F32),
            pltpu.VMEM((COLD, RANK), F32),
            dma((9,)),
            dma((2,)),
            dma((6, 2)),
            dma((2, 2)),
            dma((2, 2)),
            dma((3, 4)),
            dma((4,)),
        ],
        compiler_params=pltpu.CompilerParams(
            collective_id=0, has_side_effects=True, vmem_limit_bytes=58 << 20
        ),
    )(users, confidence, item_lists, block_counts, requests, hot_factors, cold_factors)
    return pl.pallas_call(
        hand_over,
        out_shape=outs,
    )(*results)


def solution(mesh):
    both = ("wide", "narrow")
    placed = (
        P(both, None),
        P(both, None, None),
        P(both, None),
        P(both),
        P(both, None),
        P(),
        P(both, None),
    )
    return jax.shard_map(
        body,
        mesh=mesh,
        in_specs=placed,
        out_specs=(P(), P(both, None)),
        check_vma=False,
    )
```

```python
import functools

import jax
import jax.numpy as jnp
from jax import lax
from jax.experimental import pallas as pl
from jax.experimental.pallas import tpu as pltpu
from jax.sharding import PartitionSpec as P

MESH = pl.DeviceIdType.MESH
REGULAR = 1.0
EPS = 1e-06
F32 = jnp.float32
BF = jnp.bfloat16
NDEV = 128
NCHIP = 64
RANK = 128
USERS = 2048
BLOCKS = 16
LENGTH = 512
HOT = 1024
HALF = 512
COLD = 512
TABLE = 1536
OWN = 8
CAP = 4
ROWS = 256
PIECE = 256
EARLY = 6
COLD_EARLY = 4


def dot(a, b):
    return jnp.dot(a, b, preferred_element_type=F32)


def halves(v):
    high = v.astype(BF)
    return high, (v - high.astype(F32)).astype(BF)


def turn(a):
    return 2 - a + 3 * (a // 2) - 2 * ((a + 1) // 4)


def kernel(
    users_in, conf_in, lists_in, counts_in, reqs_in, hot_in, cold_in,
    hot_out, cold_out,
    users, conf, lists, counts, reqs, hot, cold, users_t, stack, lmat, cmat, pick, place,
    send0, recv0, first_send, first_recv, gram2,
    csend, crecv,
    sib_out, sib_in, hsend, hrecv, hdir, scal,
    q_part, q_in, q_sum, q_recv,
    cold_sol, cold_res, cold_dir, cold_image,
    insem, sem0, csem, sibsem, hsem, fsem, qsem,
):
    w = lax.axis_index("wide")
    y = lax.axis_index("narrow")
    z = w // 8
    x = (w // 2) % 4
    k = w % 2
    me = w * 4 + y
    chip = (z * 4 + x) * 4 + y
    sibling = (w + 1 - 2 * k, y)

    ys = [lax.rem(y + d, 4) for d in (2, 1, 3, 0)]

    def each_chip(fn):
        def planes(a, carry):
            z2 = lax.rem(z + turn(a), 4)

            def rows(b, inner):
                zx = z2 * 4 + lax.rem(x + turn(b), 4)
                here = jnp.logical_and(a == 3, b == 3)
                for place_at, y2 in enumerate(ys):
                    fn(zx, y2, here if place_at == 3 else None)
                return inner

            return lax.fori_loop(0, 4, rows, carry)

        lax.fori_loop(0, 4, planes, 0)

    def each_other(fn):
        def both_cores(zx, y2, here):
            for core in (1 - k, k):
                w2 = zx * 2 + core
                if here is None or core is not k:
                    fn((w2, y2), w2 * 4 + y2)
                else:
                    pl.when(jnp.logical_not(here))(lambda: fn((w2, y2), w2 * 4 + y2))

        each_chip(both_cores)

    def each_same_core(fn):
        def one(zx, y2, here):
            if here is None:
                fn((zx * 2 + k, y2), zx * 4 + y2)
            else:
                pl.when(jnp.logical_not(here))(lambda: fn((zx * 2 + k, y2), zx * 4 + y2))

        each_chip(one)

    def loop(count, fn, unroll=1):
        def step(t, carry):
            fn(t)
            return carry

        lax.fori_loop(0, count, step, 0, unroll=unroll)

    def push(src, dst, send, recv, device):
        pltpu.make_async_remote_copy(
            src_ref=src, dst_ref=dst, send_sem=send, recv_sem=recv,
            device_id=device, device_id_type=MESH,
        ).start()

    def wait(ref, sem):
        pltpu.make_async_copy(ref, ref, sem).wait()

    loads = [
        pltpu.make_async_copy(src, dst, insem.at[i])
        for i, (src, dst) in enumerate(
            (
                (users_in, users), (conf_in, conf), (hot_in, hot), (cold_in, cold),
                (reqs_in, reqs), (lists_in, lists), (counts_in, counts),
            )
        )
    ]
    for load in loads:
        load.start()
    barrier = pltpu.get_barrier_semaphore()

    def greet(device, _):
        pl.semaphore_signal(barrier, inc=1, device_id=device, device_id_type=MESH)

    each_other(greet)

    loads[4].wait()
    owner_of = lax.broadcasted_iota(jnp.int32, (NDEV, COLD), 0)
    entry = lax.broadcasted_iota(jnp.int32, (NDEV, COLD), 1)
    mine = jnp.where((entry >> 2) == owner_of, reqs[...].astype(F32), 0.0)
    lanes_of = (
        (lax.broadcasted_iota(jnp.int32, (COLD, 128), 0) & 3)
        == lax.broadcasted_iota(jnp.int32, (COLD, 128), 1)
    )
    lane_pick = lanes_of.astype(F32).astype(BF)
    high, low = halves(mine)
    asked = dot(high, lane_pick) + dot(low, lane_pick)
    send0[:, 0:1, :] = asked.reshape(NDEV, 1, 128)
    loads[0].wait()
    for b in range(BLOCKS):
        users_t[:, b * 128:(b + 1) * 128] = users[b * 128:(b + 1) * 128, :].T
    send0[:, 1:2, :] = dot(users_t[...], users[...]).reshape(NDEV, 1, 128)
    loads[1].wait()
    loads[5].wait()
    loads[6].wait()

    def fold(b, first, last, shift):
        listed = lists[pl.ds(b, 1), :]
        column = pl.ds(pl.multiple_of(b * 128, 128), 128)
        row = lax.broadcasted_iota(jnp.int32, (ROWS, LENGTH), 0).astype(F32).astype(BF)
        for base in range(first, last, ROWS):
            near = jnp.clip(listed - base, -1, ROWS).astype(F32).astype(BF)
            chosen = jnp.where(row == near, jnp.ones((), BF), jnp.zeros((), BF))
            both = dot(chosen, stack[b])
            level_sum = both[:, :128]
            lmat[base:base + ROWS, column] = level_sum.astype(BF)
            cmat[base:base + ROWS, column] = (level_sum - both[:, 128:] + shift).astype(BF)

    def fold_hot(b):
        used = lax.broadcasted_iota(jnp.int32, (LENGTH, 128), 0) < counts[b]
        level = jnp.where(used, conf[b].T.astype(F32), 0.0)
        clicked = jnp.where(level > 0.0, 1.0, 0.0)
        stack[b, :, :128] = level.astype(BF)
        stack[b, :, 128:] = clicked.astype(BF)
        fold(b, 0, HOT, 1.0)

    def fold_cold(b):
        fold(b, HOT, TABLE, 0.0)

    loop(EARLY, fold_hot, unroll=2)
    pl.semaphore_wait(barrier, NDEV - 1)

    def send_request(device, s2):
        push(send0.at[s2], recv0.at[me], sem0.at[0], sem0.at[1], device)

    each_other(send_request)
    recv0[pl.ds(me, 1)] = send0[pl.ds(me, 1)]

    def fold_late(b):
        fold_hot(b + EARLY)

    loop(BLOCKS - EARLY, fold_late, unroll=2)
    loop(COLD_EARLY, fold_cold, unroll=4)

    def cold_exchange(e, rows):
        csend[e] = rows.reshape(NDEV, CAP, 128)

        def go(device, s2):
            push(csend.at[e, s2], crecv.at[e, me], csem.at[e, 0], csem.at[e, 1], device)

        each_other(go)
        crecv[e, pl.ds(me, 1)] = csend[e, pl.ds(me, 1)]

    def cold_arrived(e):
        wait(crecv.at[e, pl.ds(0, NDEV - 1)], csem.at[e, 1])
        return crecv[e].reshape(COLD, 128)

    def cold_fetch(e, values):
        cold_exchange(e, dot(pick[...], values.astype(BF)))

    def cold_placed(e):
        high, low = halves(cold_arrived(e))
        both = dot(place[...], jnp.concatenate([high, low], axis=1))
        return both[:, :128] + both[:, 128:]

    def user_terms(table, base, opening):
        rows = pl.ds(base, HALF)
        total = jnp.zeros((HALF, RANK), F32)
        for at in range(0, USERS, PIECE):
            scores = dot(table, users_t[:, at:at + PIECE])
            weight = cmat[rows, at:at + PIECE].astype(F32) * scores
            if opening:
                weight = lmat[rows, at:at + PIECE].astype(F32) - weight
            total = total + dot(weight.astype(BF), users[at:at + PIECE, :])
        return total

    def user_squares(table, base):
        rows = pl.ds(base, HALF)
        total = jnp.zeros((HALF, 128), F32)
        for at in range(0, USERS, PIECE):
            scores = dot(table, users_t[:, at:at + PIECE])
            part = cmat[rows, at:at + PIECE].astype(F32) * scores * scores
            for lane in range(0, PIECE, 128):
                total = total + part[:, lane:lane + 128]
        return total

    other_base = (1 - k) * HALF
    own_base = k * HALF

    def hot_give_sibling(g, read_table, opening):
        base = pl.multiple_of(other_base, HALF)
        sib_out[g] = user_terms(read_table(base), base, opening)
        push(sib_out.at[g], sib_in.at[g], sibsem.at[g, 0], sibsem.at[g, 1], sibling)

    def hot_give_own(g, read_table, opening):
        base = pl.multiple_of(own_base, HALF)
        hsend[g] = user_terms(read_table(base), base, opening)

    def hot_give(g):
        wait(sib_in.at[g], sibsem.at[g, 1])
        hsend[g] = hsend[g] + sib_in[g]

        def go(device, c2):
            push(
                hsend.at[g, pl.ds(pl.multiple_of(c2 * OWN, OWN), OWN)], hrecv.at[g, chip],
                hsem.at[g, 0], hsem.at[g, 1], device,
            )

        each_same_core(go)
        hrecv[g, pl.ds(chip, 1)] = hsend[
            g, pl.ds(pl.multiple_of(chip * OWN, OWN), OWN), :
        ].reshape(1, OWN, 128)

    def hot_given(g):
        wait(hrecv.at[g, pl.ds(0, NCHIP - 1)], hsem.at[g, 1])
        return jnp.sum(hrecv[g], axis=0)

    own_rows = pl.ds(pl.multiple_of(own_base + chip * OWN, OWN), OWN)
    own_half = pl.ds(pl.multiple_of(own_base, HALF), HALF)

    def hot_spread(buf, f, values):
        buf[own_rows, :] = values

        def go(device, _):
            push(buf.at[own_rows], buf.at[own_rows], fsem.at[f, 0], fsem.at[f, 1], device)

        each_same_core(go)

    def hot_forward(buf, f):
        wait(buf.at[pl.ds(0, (NCHIP - 1) * OWN)], fsem.at[f, 1])
        push(buf.at[own_half], buf.at[own_half], fsem.at[f, 2], fsem.at[f, 3], sibling)

    def hot_forwarded(buf, f):
        wait(buf.at[pl.ds(0, HALF)], fsem.at[f, 3])

    def read_rows(buf):
        return lambda base: buf[pl.ds(base, HALF), :].astype(BF)

    def cold_give(e, table, opening):
        cold_exchange(e, user_terms(table.astype(BF), HOT, opening))

    def apply_gram(v):
        high, low = halves(v)
        return dot(high, gram2[0]) + dot(high, gram2[1]) + dot(low, gram2[0]) + REGULAR * v

    def row_sum(v):
        return jnp.sum(v, axis=1, keepdims=True)

    wait(recv0.at[pl.ds(0, NDEV - 1)], sem0.at[1])
    high, low = halves(recv0[:, 0:1, :].reshape(NDEV, 128))
    spread = (
        (lax.broadcasted_iota(jnp.int32, (COLD, NDEV), 0) >> 2)
        == lax.broadcasted_iota(jnp.int32, (COLD, NDEV), 1)
    ).astype(F32).astype(BF)
    rows4 = jnp.where(lanes_of, dot(spread, high) + dot(spread, low), 0.0)
    wanted_col = row_sum(rows4).astype(jnp.int32)
    lane_item = lax.broadcasted_iota(jnp.int32, (COLD, COLD), 1)
    pick[...] = jnp.where(wanted_col == lane_item, 1.0, 0.0).astype(BF)
    loads[3].wait()
    first_send[:, 0:CAP, :] = dot(pick[...], cold[...].astype(BF)).reshape(NDEV, CAP, 128)
    gram_row = jnp.sum(recv0[:, 1:2, :], axis=0, keepdims=True)
    first_send[:, CAP:, :] = jnp.broadcast_to(gram_row, (NDEV, 1, 128))

    def send_first(device, s2):
        push(first_send.at[s2], first_recv.at[me], csem.at[0, 0], csem.at[0, 1], device)

    each_other(send_first)
    first_recv[pl.ds(me, 1)] = first_send[pl.ds(me, 1)]
    wanted_wide = jnp.broadcast_to(wanted_col, (COLD, 128))
    wanted_row = wanted_wide.astype(F32).T[0:1, :].astype(jnp.int32)
    row_item = lax.broadcasted_iota(jnp.int32, (COLD, COLD), 0)
    place[...] = jnp.where(wanted_row == row_item, 1.0, 0.0).astype(BF)

    loads[2].wait()
    hot_give_sibling(0, read_rows(hot), True)
    hot_give_own(0, read_rows(hot), True)
    hot_give(0)
    loop(BLOCKS - COLD_EARLY, lambda b: fold_cold(b + COLD_EARLY), unroll=4)

    wait(first_recv.at[pl.ds(0, NDEV - 1)], csem.at[0, 1])
    cold_give(1, first_recv[:, 0:CAP, :].reshape(COLD, 128), True)

    hot_res = hot_given(0) - REGULAR * hot[own_rows, :]
    hot_dir = hot_res
    hot_norm = row_sum(hot_res * hot_res)
    hdir0 = hdir.at[0]
    hdir1 = hdir.at[1]
    hot_spread(hdir0, 0, hot_dir)

    gram2[0], gram2[1] = halves(first_recv[:, CAP:, :].reshape(RANK, RANK))
    cold_image[...] = apply_gram(cold[...])
    residual = cold_placed(1) - cold_image[...]
    cold_res[...] = residual
    cold_fetch(2, residual)
    cold_norm = row_sum(residual * residual)
    cold_image[...] = apply_gram(residual)
    cold_curve = row_sum(residual * cold_image[...])

    hot_forward(hdir0, 0)
    hot_give_own(1, read_rows(hdir0), False)
    hot_forwarded(hdir0, 0)
    hot_give_sibling(1, read_rows(hdir0), False)
    hot_give(1)
    cold_give(3, cold_arrived(2), False)

    image = hot_given(1) + REGULAR * hot_dir
    hot_alpha = hot_norm / (row_sum(hot_dir * image) + EPS)
    hot_res = hot_res - hot_alpha * image
    fresh = row_sum(hot_res * hot_res)
    hot_dir = hot_res + fresh / (hot_norm + EPS) * hot_dir
    hot_spread(hdir1, 1, hot_dir)
    lane = lax.broadcasted_iota(jnp.int32, (OWN, 128), 1)
    scal_own = jnp.where(lane < 64, hot_alpha, fresh)

    term = cold_placed(3)
    old = cold_res[...]
    cold_alpha = cold_norm / (row_sum(old * term) + cold_curve + EPS)
    residual = old - cold_alpha * (term + cold_image[...])
    fresh = row_sum(residual * residual)
    direction = residual + fresh / (cold_norm + EPS) * old
    cold_fetch(4, direction)
    cold_sol[...] = cold[...] + cold_alpha * old
    cold_dir[...] = direction
    cold_norm = fresh
    cold_curve = row_sum(direction * apply_gram(direction))
    hot_spread(scal, 2, scal_own)

    hot_forward(hdir1, 1)

    def hot_squares(base):
        start = pl.multiple_of(base, HALF)
        square = user_squares(hdir[1, pl.ds(start, HALF), :].astype(BF), start)
        for j in range(HALF // 128):
            q_part[pl.ds(start // 128 + j, 1), :] = jnp.sum(
                square[j * 128:(j + 1) * 128, :].T, axis=0, keepdims=True
            )

    hot_squares(own_base)
    hot_forwarded(hdir1, 1)
    hot_squares(other_base)
    push(q_part, q_in, qsem.at[0], qsem.at[1], sibling)
    wait(q_in, qsem.at[1])
    q_sum[...] = q_part[...] + q_in[...]

    def send_q(device, _):
        push(q_sum, q_recv.at[chip], qsem.at[2], qsem.at[3], device)

    each_same_core(send_q)
    q_recv[pl.ds(chip, 1)] = q_sum[...].reshape(1, OWN, 128)

    cold_exchange(5, user_squares(cold_arrived(4).astype(BF), HOT))

    hot_forward(scal, 2)
    hot_forwarded(scal, 2)
    curves = []
    for a in range(HOT // 128):
        rows = slice(a * 128, (a + 1) * 128)
        d1 = hdir[1, rows, :]
        curves.append(REGULAR * row_sum(d1 * d1) + EPS)
        hot_out[rows, :] = hot[rows, :] + scal[rows, 0:1] * hdir[0, rows, :]
    wait(q_recv.at[pl.ds(0, NCHIP - 1)], qsem.at[3])
    q_col = jnp.sum(q_recv[...], axis=0).T
    for a in range(HOT // 128):
        rows = slice(a * 128, (a + 1) * 128)
        alpha = scal[rows, 64:65] / (q_col[:, a:a + 1] + curves[a])
        hot_out[rows, :] = hot_out[rows, :] + alpha * hdir[1, rows, :]

    alpha = cold_norm / (row_sum(cold_placed(5)) + cold_curve + EPS)
    cold_out[...] = cold_sol[...] + alpha * cold_dir[...]

    wait(send0.at[pl.ds(0, NDEV - 1)], sem0.at[0])

    wait(first_send.at[pl.ds(0, NDEV - 1)], csem.at[0, 0])
    for e in range(1, 6):
        wait(csend.at[e, pl.ds(0, NDEV - 1)], csem.at[e, 0])
    for g in range(2):
        wait(sib_out.at[g], sibsem.at[g, 0])
        wait(hrecv.at[g, pl.ds(0, NCHIP - 1)], hsem.at[g, 0])
    for f in range(3):
        wait(hrecv.at[0, pl.ds(0, NCHIP - 1)], fsem.at[f, 0])
        wait(scal.at[pl.ds(0, HALF)], fsem.at[f, 2])
    wait(q_part, qsem.at[0])
    wait(q_recv.at[pl.ds(0, NCHIP - 1)], qsem.at[2])


def hand_over(hot_in, cold_in, hot_out, cold_out):
    hot_out[...] = hot_in[...]
    cold_out[...] = cold_in[...]


def body(users, confidence, item_lists, block_counts, requests, hot_factors, cold_factors):
    hbm = pl.BlockSpec(memory_space=pl.ANY)
    dma = pltpu.SemaphoreType.DMA
    outs = (
        jax.ShapeDtypeStruct((HOT, RANK), F32),
        jax.ShapeDtypeStruct((COLD, RANK), F32),
    )
    vmem = pl.BlockSpec(memory_space=pltpu.VMEM)
    results = pl.pallas_call(
        kernel,
        out_shape=(pltpu.VMEM((HOT, RANK), F32), pltpu.VMEM((COLD, RANK), F32)),
        in_specs=[hbm] * 7,
        out_specs=(vmem, vmem),
        scratch_shapes=[
            pltpu.VMEM((USERS, RANK), BF),
            pltpu.VMEM((BLOCKS, 128, LENGTH), BF),
            pltpu.VMEM((BLOCKS, LENGTH), jnp.int32),
            pltpu.SMEM((BLOCKS,), jnp.int32),
            pltpu.VMEM((1, COLD), jnp.int32),
            pltpu.VMEM((HOT, RANK), F32),
            pltpu.VMEM((COLD, RANK), F32),
            pltpu.VMEM((RANK, USERS), BF),
            pltpu.VMEM((BLOCKS, LENGTH, 256), BF),
            pltpu.VMEM((TABLE, USERS), BF),
            pltpu.VMEM((TABLE, USERS), BF),
            pltpu.VMEM((COLD, COLD), BF),
            pltpu.VMEM((COLD, COLD), BF),
            pltpu.VMEM((NDEV, 2, 128), F32),
            pltpu.VMEM((NDEV, 2, 128), F32),
            pltpu.VMEM((NDEV, CAP + 1, 128), F32),
            pltpu.VMEM((NDEV, CAP + 1, 128), F32),
            pltpu.VMEM((2, RANK, RANK), BF),
            pltpu.VMEM((6, NDEV, CAP, 128), F32),
            pltpu.VMEM((6, NDEV, CAP, 128), F32),
            pltpu.VMEM((2, HALF, 128), F32),
            pltpu.VMEM((2, HALF, 128), F32),
            pltpu.VMEM((2, HALF, 128), F32),
            pltpu.VMEM((2, NCHIP, OWN, 128), F32),
            pltpu.VMEM((2, HOT, 128), F32),
            pltpu.VMEM((HOT, 128), F32),
            pltpu.VMEM((OWN, 128), F32),
            pltpu.VMEM((OWN, 128), F32),
            pltpu.VMEM((OWN, 128), F32),
            pltpu.VMEM((NCHIP, OWN, 128), F32),
            pltpu.VMEM((COLD, RANK), F32),
            pltpu.VMEM((COLD, RANK), F32),
            pltpu.VMEM((COLD, RANK), F32),
            pltpu.VMEM((COLD, RANK), F32),
            dma((7,)),
            dma((2,)),
            dma((6, 2)),
            dma((2, 2)),
            dma((2, 2)),
            dma((3, 4)),
            dma((4,)),
        ],
        compiler_params=pltpu.CompilerParams(
            collective_id=0, has_side_effects=True, vmem_limit_bytes=58 << 20
        ),
    )(users, confidence, item_lists, block_counts, requests, hot_factors, cold_factors)
    return pl.pallas_call(
        hand_over,
        out_shape=outs,
        in_specs=[vmem, vmem],
        out_specs=(vmem, vmem),
    )(*(pltpu.with_memory_space_constraint(r, pltpu.VMEM) for r in results))


def solution(mesh):
    both = ("wide", "narrow")
    placed = (
        P(both, None),
        P(both, None, None),
        P(both, None),
        P(both),
        P(both, None),
        P(),
        P(both, None),
    )
    return jax.shard_map(
        body,
        mesh=mesh,
        in_specs=placed,
        out_specs=(P(), P(both, None)),
        check_vma=False,
    )
```

```python
import functools

import jax
import jax.numpy as jnp
from jax import lax
from jax.experimental import pallas as pl
from jax.experimental.pallas import tpu as pltpu
from jax.sharding import PartitionSpec as P

MESH = pl.DeviceIdType.MESH
REGULAR = 1.0
EPS = 1e-06
F32 = jnp.float32
BF = jnp.bfloat16
NDEV = 128
NCHIP = 64
RANK = 128
USERS = 2048
BLOCKS = 16
LENGTH = 512
HOT = 1024
HALF = 512
COLD = 512
TABLE = 1536
OWN = 8
CAP = 4
ROWS = 256
PIECE = 256
EARLY = 6
COLD_EARLY = 4


def dot(a, b):
    return jnp.dot(a, b, preferred_element_type=F32)


def halves(v):
    high = v.astype(BF)
    return high, (v - high.astype(F32)).astype(BF)


def turn(a):
    return 2 - a + 3 * (a // 2) - 2 * ((a + 1) // 4)


def kernel(
    users_in, conf_in, lists_in, counts_in, reqs_in, hot_in, cold_in,
    hot_out, cold_out,
    users, conf, lists, counts, reqs, hot, cold, users_t, stack, lmat, cmat, pick, place,
    send0, recv0, first_send, first_recv, gram2,
    csend, crecv,
    sib_out, sib_in, hsend, hrecv, hdir, scal,
    q_part, q_in, q_sum, q_recv,
    cold_sol, cold_res, cold_dir, cold_image, ctable,
    insem, sem0, csem, sibsem, hsem, fsem, qsem,
):
    w = lax.axis_index("wide")
    y = lax.axis_index("narrow")
    z = w // 8
    x = (w // 2) % 4
    k = w % 2
    me = w * 4 + y
    chip = (z * 4 + x) * 4 + y
    sibling = (w + 1 - 2 * k, y)

    ys = [lax.rem(y + d, 4) for d in (2, 1, 3, 0)]

    def each_chip(fn):
        def planes(a, carry):
            z2 = lax.rem(z + turn(a), 4)

            def rows(b, inner):
                zx = z2 * 4 + lax.rem(x + turn(b), 4)
                here = jnp.logical_and(a == 3, b == 3)
                for place_at, y2 in enumerate(ys):
                    fn(zx, y2, here if place_at == 3 else None)
                return inner

            return lax.fori_loop(0, 4, rows, carry)

        lax.fori_loop(0, 4, planes, 0)

    far, near = lax.rem(z + 2, 4), z + 1 - 2 * lax.rem(z, 2)
    far_half = 1 - z // 2

    def each_of_half(fn, start, end, own):
        def planes(a, carry):
            z2 = start + a * (end - start)

            def rows(b, inner):
                zx = z2 * 4 + lax.rem(x + turn(b), 4)
                here = jnp.logical_and(a == 1, b == 3)
                for place_at, y2 in enumerate(ys):
                    for core in (1 - k, k):
                        w2 = zx * 2 + core
                        if own and place_at == 3 and core is k:
                            pl.when(jnp.logical_not(here))(
                                lambda: fn((w2, y2), w2 * 4 + y2)
                            )
                        else:
                            fn((w2, y2), w2 * 4 + y2)
                return inner

            return lax.fori_loop(0, 4, rows, carry)

        lax.fori_loop(0, 2, planes, 0)

    def each_other(fn):
        def both_cores(zx, y2, here):
            for core in (1 - k, k):
                w2 = zx * 2 + core
                if here is None or core is not k:
                    fn((w2, y2), w2 * 4 + y2)
                else:
                    pl.when(jnp.logical_not(here))(lambda: fn((w2, y2), w2 * 4 + y2))

        each_chip(both_cores)

    def each_same_core(fn):
        def one(zx, y2, here):
            if here is None:
                fn((zx * 2 + k, y2), zx * 4 + y2)
            else:
                pl.when(jnp.logical_not(here))(lambda: fn((zx * 2 + k, y2), zx * 4 + y2))

        each_chip(one)

    def loop(count, fn, unroll=1):
        def step(t, carry):
            fn(t)
            return carry

        lax.fori_loop(0, count, step, 0, unroll=unroll)

    def push(src, dst, send, recv, device):
        pltpu.make_async_remote_copy(
            src_ref=src, dst_ref=dst, send_sem=send, recv_sem=recv,
            device_id=device, device_id_type=MESH,
        ).start()

    def wait(ref, sem):
        pltpu.make_async_copy(ref, ref, sem).wait()

    loads = [
        pltpu.make_async_copy(src, dst, insem.at[i])
        for i, (src, dst) in enumerate(
            (
                (users_in, users), (conf_in, conf), (hot_in, hot), (cold_in, cold),
                (reqs_in, reqs), (lists_in, lists), (counts_in, counts),
            )
        )
    ]
    for load in loads:
        load.start()
    barrier = pltpu.get_barrier_semaphore()

    def greet(device, _):
        pl.semaphore_signal(barrier, inc=1, device_id=device, device_id_type=MESH)

    each_other(greet)

    loads[4].wait()
    owner_of = lax.broadcasted_iota(jnp.int32, (NDEV, COLD), 0)
    entry = lax.broadcasted_iota(jnp.int32, (NDEV, COLD), 1)
    mine = jnp.where((entry >> 2) == owner_of, reqs[...].astype(F32), 0.0)
    lanes_of = (
        (lax.broadcasted_iota(jnp.int32, (COLD, 128), 0) & 3)
        == lax.broadcasted_iota(jnp.int32, (COLD, 128), 1)
    )
    lane_pick = lanes_of.astype(F32).astype(BF)
    high, low = halves(mine)
    asked = dot(high, lane_pick) + dot(low, lane_pick)
    send0[:, 0:1, :] = asked.reshape(NDEV, 1, 128)
    loads[0].wait()
    for b in range(BLOCKS):
        users_t[:, b * 128:(b + 1) * 128] = users[b * 128:(b + 1) * 128, :].T
    send0[:, 1:2, :] = dot(users_t[...], users[...]).reshape(NDEV, 1, 128)
    loads[1].wait()
    loads[5].wait()
    loads[6].wait()

    def fold(b, first, last, shift):
        listed = lists[pl.ds(b, 1), :]
        column = pl.ds(pl.multiple_of(b * 128, 128), 128)
        row = lax.broadcasted_iota(jnp.int32, (ROWS, LENGTH), 0).astype(F32).astype(BF)
        for base in range(first, last, ROWS):
            near = jnp.clip(listed - base, -1, ROWS).astype(F32).astype(BF)
            chosen = jnp.where(row == near, jnp.ones((), BF), jnp.zeros((), BF))
            both = dot(chosen, stack[b])
            level_sum = both[:, :128]
            lmat[base:base + ROWS, column] = level_sum.astype(BF)
            cmat[base:base + ROWS, column] = (level_sum - both[:, 128:] + shift).astype(BF)

    def fold_hot(b):
        used = lax.broadcasted_iota(jnp.int32, (LENGTH, 128), 0) < counts[b]
        level = jnp.where(used, conf[b].T.astype(F32), 0.0)
        clicked = jnp.where(level > 0.0, 1.0, 0.0)
        stack[b, :, :128] = level.astype(BF)
        stack[b, :, 128:] = clicked.astype(BF)
        fold(b, 0, HOT, 1.0)

    def fold_cold(b):
        fold(b, HOT, TABLE, 0.0)

    loop(EARLY, fold_hot, unroll=2)
    pl.semaphore_wait(barrier, NDEV - 1)

    def send_request(device, s2):
        push(send0.at[s2], recv0.at[me], sem0.at[0], sem0.at[1], device)

    each_other(send_request)
    recv0[pl.ds(me, 1)] = send0[pl.ds(me, 1)]

    def fold_late(b):
        fold_hot(b + EARLY)

    loop(BLOCKS - EARLY, fold_late, unroll=2)
    loop(COLD_EARLY, fold_cold, unroll=4)

    def cold_exchange(e, rows):
        csend[e] = rows.reshape(NDEV, CAP, 128)

        def go(device, s2):
            push(csend.at[e, s2], crecv.at[e, me], csem.at[e, 0], csem.at[e, 1], device)

        each_other(go)
        crecv[e, pl.ds(me, 1)] = csend[e, pl.ds(me, 1)]

    def cold_arrived(e):
        wait(crecv.at[e, pl.ds(0, NDEV - 1)], csem.at[e, 1])
        return crecv[e].reshape(COLD, 128)

    def cold_fetch(e, values):
        cold_exchange(e, dot(pick[...], values.astype(BF)))

    def cold_placed(e):
        high, low = halves(cold_arrived(e))
        both = dot(place[...], jnp.concatenate([high, low], axis=1))
        return both[:, :128] + both[:, 128:]

    def user_terms(table, base, opening):
        rows = pl.ds(base, table.shape[0])
        total = jnp.zeros((table.shape[0], RANK), F32)
        for at in range(0, USERS, PIECE):
            scores = dot(table, users_t[:, at:at + PIECE])
            weight = cmat[rows, at:at + PIECE].astype(F32) * scores
            if opening:
                weight = lmat[rows, at:at + PIECE].astype(F32) - weight
            total = total + dot(weight.astype(BF), users[at:at + PIECE, :])
        return total

    def user_squares(table, base):
        rows = pl.ds(base, HALF)
        total = jnp.zeros((HALF, 128), F32)
        for at in range(0, USERS, PIECE):
            scores = dot(table, users_t[:, at:at + PIECE])
            part = cmat[rows, at:at + PIECE].astype(F32) * scores * scores
            for lane in range(0, PIECE, 128):
                total = total + part[:, lane:lane + 128]
        return total

    other_base = (1 - k) * HALF
    own_base = k * HALF

    def hot_give_sibling(g, read_table, opening):
        base = pl.multiple_of(other_base, HALF)
        sib_out[g] = user_terms(read_table(base), base, opening)
        push(sib_out.at[g], sib_in.at[g], sibsem.at[g, 0], sibsem.at[g, 1], sibling)

    def hot_give_own(g, read_table, opening):
        base = pl.multiple_of(own_base, HALF)
        hsend[g] = user_terms(read_table(base), base, opening)

    def hot_give(g):
        wait(sib_in.at[g], sibsem.at[g, 1])
        hsend[g] = hsend[g] + sib_in[g]

        def go(device, c2):
            push(
                hsend.at[g, pl.ds(pl.multiple_of(c2 * OWN, OWN), OWN)], hrecv.at[g, chip],
                hsem.at[g, 0], hsem.at[g, 1], device,
            )

        each_same_core(go)
        hrecv[g, pl.ds(chip, 1)] = hsend[
            g, pl.ds(pl.multiple_of(chip * OWN, OWN), OWN), :
        ].reshape(1, OWN, 128)

    def hot_given(g):
        wait(hrecv.at[g, pl.ds(0, NCHIP - 1)], hsem.at[g, 1])
        return jnp.sum(hrecv[g], axis=0)

    own_rows = pl.ds(pl.multiple_of(own_base + chip * OWN, OWN), OWN)
    own_half = pl.ds(pl.multiple_of(own_base, HALF), HALF)

    def hot_spread(buf, f, values):
        buf[own_rows, :] = values

        def go(device, _):
            push(buf.at[own_rows], buf.at[own_rows], fsem.at[f, 0], fsem.at[f, 1], device)

        each_same_core(go)

    def hot_forward(buf, f):
        wait(buf.at[pl.ds(0, (NCHIP - 1) * OWN)], fsem.at[f, 1])
        push(buf.at[own_half], buf.at[own_half], fsem.at[f, 2], fsem.at[f, 3], sibling)

    def hot_forwarded(buf, f):
        wait(buf.at[pl.ds(0, HALF)], fsem.at[f, 3])

    def read_rows(buf):
        return lambda base: buf[pl.ds(base, HALF), :].astype(BF)

    def cold_give(e, table, opening):
        ctable[...] = table.astype(BF)

        def go(device, s2):
            push(csend.at[e, s2], crecv.at[e, me], csem.at[e, 0], csem.at[e, 1], device)

        for half, start, end, own in (
            (far_half, far, 3 - z, False), (1 - far_half, near, z, True),
        ):
            local = pl.multiple_of(half * ROWS, ROWS)
            rows = ctable[pl.ds(local, ROWS), :]
            csend[e, pl.ds(half * (NDEV // 2), NDEV // 2)] = user_terms(
                rows, pl.multiple_of(HOT + half * ROWS, ROWS), opening
            ).reshape(NDEV // 2, CAP, 128)
            each_of_half(go, start, end, own)
        crecv[e, pl.ds(me, 1)] = csend[e, pl.ds(me, 1)]

    def apply_gram(v):
        high, low = halves(v)
        return dot(high, gram2[0]) + dot(high, gram2[1]) + dot(low, gram2[0]) + REGULAR * v

    def row_sum(v):
        return jnp.sum(v, axis=1, keepdims=True)

    wait(recv0.at[pl.ds(0, NDEV - 1)], sem0.at[1])
    high, low = halves(recv0[:, 0:1, :].reshape(NDEV, 128))
    spread = (
        (lax.broadcasted_iota(jnp.int32, (COLD, NDEV), 0) >> 2)
        == lax.broadcasted_iota(jnp.int32, (COLD, NDEV), 1)
    ).astype(F32).astype(BF)
    rows4 = jnp.where(lanes_of, dot(spread, high) + dot(spread, low), 0.0)
    wanted_col = row_sum(rows4).astype(jnp.int32)
    lane_item = lax.broadcasted_iota(jnp.int32, (COLD, COLD), 1)
    pick[...] = jnp.where(wanted_col == lane_item, 1.0, 0.0).astype(BF)
    loads[3].wait()
    first_send[:, 0:CAP, :] = dot(pick[...], cold[...].astype(BF)).reshape(NDEV, CAP, 128)
    gram_row = jnp.sum(recv0[:, 1:2, :], axis=0, keepdims=True)
    first_send[:, CAP:, :] = jnp.broadcast_to(gram_row, (NDEV, 1, 128))

    def send_first(device, s2):
        push(first_send.at[s2], first_recv.at[me], csem.at[0, 0], csem.at[0, 1], device)

    each_other(send_first)
    first_recv[pl.ds(me, 1)] = first_send[pl.ds(me, 1)]
    wanted_wide = jnp.broadcast_to(wanted_col, (COLD, 128))
    wanted_row = wanted_wide.astype(F32).T[0:1, :].astype(jnp.int32)
    row_item = lax.broadcasted_iota(jnp.int32, (COLD, COLD), 0)
    place[...] = jnp.where(wanted_row == row_item, 1.0, 0.0).astype(BF)

    loads[2].wait()
    hot_give_sibling(0, read_rows(hot), True)
    hot_give_own(0, read_rows(hot), True)
    hot_give(0)
    loop(BLOCKS - COLD_EARLY, lambda b: fold_cold(b + COLD_EARLY), unroll=4)

    wait(first_recv.at[pl.ds(0, NDEV - 1)], csem.at[0, 1])
    cold_give(1, first_recv[:, 0:CAP, :].reshape(COLD, 128), True)

    hot_res = hot_given(0) - REGULAR * hot[own_rows, :]
    hot_dir = hot_res
    hot_norm = row_sum(hot_res * hot_res)
    hdir0 = hdir.at[0]
    hdir1 = hdir.at[1]
    hot_spread(hdir0, 0, hot_dir)

    gram2[0], gram2[1] = halves(first_recv[:, CAP:, :].reshape(RANK, RANK))
    cold_image[...] = apply_gram(cold[...])
    residual = cold_placed(1) - cold_image[...]
    cold_res[...] = residual
    cold_fetch(2, residual)
    cold_norm = row_sum(residual * residual)
    cold_image[...] = apply_gram(residual)
    cold_curve = row_sum(residual * cold_image[...])

    hot_forward(hdir0, 0)
    hot_give_own(1, read_rows(hdir0), False)
    hot_forwarded(hdir0, 0)
    hot_give_sibling(1, read_rows(hdir0), False)
    hot_give(1)
    cold_give(3, cold_arrived(2), False)

    image = hot_given(1) + REGULAR * hot_dir
    hot_alpha = hot_norm / (row_sum(hot_dir * image) + EPS)
    hot_res = hot_res - hot_alpha * image
    fresh = row_sum(hot_res * hot_res)
    hot_dir = hot_res + fresh / (hot_norm + EPS) * hot_dir
    hot_spread(hdir1, 1, hot_dir)
    lane = lax.broadcasted_iota(jnp.int32, (OWN, 128), 1)
    scal_own = jnp.where(lane < 64, hot_alpha, fresh)

    term = cold_placed(3)
    old = cold_res[...]
    cold_alpha = cold_norm / (row_sum(old * term) + cold_curve + EPS)
    residual = old - cold_alpha * (term + cold_image[...])
    fresh = row_sum(residual * residual)
    direction = residual + fresh / (cold_norm + EPS) * old
    cold_fetch(4, direction)
    cold_sol[...] = cold[...] + cold_alpha * old
    cold_dir[...] = direction
    cold_norm = fresh
    cold_curve = row_sum(direction * apply_gram(direction))
    hot_spread(scal, 2, scal_own)

    hot_forward(hdir1, 1)

    def hot_squares(base):
        start = pl.multiple_of(base, HALF)
        square = user_squares(hdir[1, pl.ds(start, HALF), :].astype(BF), start)
        for j in range(HALF // 128):
            q_part[pl.ds(start // 128 + j, 1), :] = jnp.sum(
                square[j * 128:(j + 1) * 128, :].T, axis=0, keepdims=True
            )

    hot_squares(own_base)
    hot_forwarded(hdir1, 1)
    hot_squares(other_base)
    push(q_part, q_in, qsem.at[0], qsem.at[1], sibling)
    wait(q_in, qsem.at[1])
    q_sum[...] = q_part[...] + q_in[...]

    def send_q(device, _):
        push(q_sum, q_recv.at[chip], qsem.at[2], qsem.at[3], device)

    each_same_core(send_q)
    q_recv[pl.ds(chip, 1)] = q_sum[...].reshape(1, OWN, 128)

    cold_exchange(5, user_squares(cold_arrived(4).astype(BF), HOT))

    hot_forward(scal, 2)
    hot_forwarded(scal, 2)
    curves = []
    for a in range(HOT // 128):
        rows = slice(a * 128, (a + 1) * 128)
        d1 = hdir[1, rows, :]
        curves.append(REGULAR * row_sum(d1 * d1) + EPS)
        hot_out[rows, :] = hot[rows, :] + scal[rows, 0:1] * hdir[0, rows, :]
    wait(q_recv.at[pl.ds(0, NCHIP - 1)], qsem.at[3])
    q_col = jnp.sum(q_recv[...], axis=0).T
    for a in range(HOT // 128):
        rows = slice(a * 128, (a + 1) * 128)
        alpha = scal[rows, 64:65] / (q_col[:, a:a + 1] + curves[a])
        hot_out[rows, :] = hot_out[rows, :] + alpha * hdir[1, rows, :]

    alpha = cold_norm / (row_sum(cold_placed(5)) + cold_curve + EPS)
    cold_out[...] = cold_sol[...] + alpha * cold_dir[...]

    wait(send0.at[pl.ds(0, NDEV - 1)], sem0.at[0])

    wait(first_send.at[pl.ds(0, NDEV - 1)], csem.at[0, 0])
    for e in range(1, 6):
        wait(csend.at[e, pl.ds(0, NDEV - 1)], csem.at[e, 0])
    for g in range(2):
        wait(sib_out.at[g], sibsem.at[g, 0])
        wait(hrecv.at[g, pl.ds(0, NCHIP - 1)], hsem.at[g, 0])
    for f in range(3):
        wait(hrecv.at[0, pl.ds(0, NCHIP - 1)], fsem.at[f, 0])
        wait(scal.at[pl.ds(0, HALF)], fsem.at[f, 2])
    wait(q_part, qsem.at[0])
    wait(q_recv.at[pl.ds(0, NCHIP - 1)], qsem.at[2])


def hand_over(hot_in, cold_in, hot_out, cold_out):
    hot_out[...] = hot_in[...]
    cold_out[...] = cold_in[...]


def body(users, confidence, item_lists, block_counts, requests, hot_factors, cold_factors):
    hbm = pl.BlockSpec(memory_space=pl.ANY)
    dma = pltpu.SemaphoreType.DMA
    outs = (
        jax.ShapeDtypeStruct((HOT, RANK), F32),
        jax.ShapeDtypeStruct((COLD, RANK), F32),
    )
    vmem = pl.BlockSpec(memory_space=pltpu.VMEM)
    results = pl.pallas_call(
        kernel,
        out_shape=(pltpu.VMEM((HOT, RANK), F32), pltpu.VMEM((COLD, RANK), F32)),
        in_specs=[hbm] * 7,
        out_specs=(vmem, vmem),
        scratch_shapes=[
            pltpu.VMEM((USERS, RANK), BF),
            pltpu.VMEM((BLOCKS, 128, LENGTH), BF),
            pltpu.VMEM((BLOCKS, LENGTH), jnp.int32),
            pltpu.SMEM((BLOCKS,), jnp.int32),
            pltpu.VMEM((1, COLD), jnp.int32),
            pltpu.VMEM((HOT, RANK), F32),
            pltpu.VMEM((COLD, RANK), F32),
            pltpu.VMEM((RANK, USERS), BF),
            pltpu.VMEM((BLOCKS, LENGTH, 256), BF),
            pltpu.VMEM((TABLE, USERS), BF),
            pltpu.VMEM((TABLE, USERS), BF),
            pltpu.VMEM((COLD, COLD), BF),
            pltpu.VMEM((COLD, COLD), BF),
            pltpu.VMEM((NDEV, 2, 128), F32),
            pltpu.VMEM((NDEV, 2, 128), F32),
            pltpu.VMEM((NDEV, CAP + 1, 128), F32),
            pltpu.VMEM((NDEV, CAP + 1, 128), F32),
            pltpu.VMEM((2, RANK, RANK), BF),
            pltpu.VMEM((6, NDEV, CAP, 128), F32),
            pltpu.VMEM((6, NDEV, CAP, 128), F32),
            pltpu.VMEM((2, HALF, 128), F32),
            pltpu.VMEM((2, HALF, 128), F32),
            pltpu.VMEM((2, HALF, 128), F32),
            pltpu.VMEM((2, NCHIP, OWN, 128), F32),
            pltpu.VMEM((2, HOT, 128), F32),
            pltpu.VMEM((HOT, 128), F32),
            pltpu.VMEM((OWN, 128), F32),
            pltpu.VMEM((OWN, 128), F32),
            pltpu.VMEM((OWN, 128), F32),
            pltpu.VMEM((NCHIP, OWN, 128), F32),
            pltpu.VMEM((COLD, RANK), F32),
            pltpu.VMEM((COLD, RANK), F32),
            pltpu.VMEM((COLD, RANK), F32),
            pltpu.VMEM((COLD, RANK), F32),
            pltpu.VMEM((COLD, RANK), BF),
            dma((7,)),
            dma((2,)),
            dma((6, 2)),
            dma((2, 2)),
            dma((2, 2)),
            dma((3, 4)),
            dma((4,)),
        ],
        compiler_params=pltpu.CompilerParams(
            collective_id=0, has_side_effects=True, vmem_limit_bytes=58 << 20
        ),
    )(users, confidence, item_lists, block_counts, requests, hot_factors, cold_factors)
    return pl.pallas_call(
        hand_over,
        out_shape=outs,
        in_specs=[vmem, vmem],
        out_specs=(vmem, vmem),
    )(*(pltpu.with_memory_space_constraint(r, pltpu.VMEM) for r in results))


def solution(mesh):
    both = ("wide", "narrow")
    placed = (
        P(both, None),
        P(both, None, None),
        P(both, None),
        P(both),
        P(both, None),
        P(),
        P(both, None),
    )
    return jax.shard_map(
        body,
        mesh=mesh,
        in_specs=placed,
        out_specs=(P(), P(both, None)),
        check_vma=False,
    )
```

```python
import functools

import jax
import jax.numpy as jnp
from jax import lax
from jax.experimental import pallas as pl
from jax.experimental.pallas import tpu as pltpu
from jax.sharding import PartitionSpec as P

MESH = pl.DeviceIdType.MESH
REGULAR = 1.0
EPS = 1e-06
F32 = jnp.float32
BF = jnp.bfloat16
NDEV = 128
NCHIP = 64
RANK = 128
USERS = 2048
BLOCKS = 16
LENGTH = 512
HOT = 1024
HALF = 512
COLD = 512
TABLE = 1536
OWN = 8
CAP = 4
ROWS = 256
PIECE = 256
EARLY = 6
COLD_EARLY = 4


def dot(a, b):
    return jnp.dot(a, b, preferred_element_type=F32)


def halves(v):
    high = v.astype(BF)
    return high, (v - high.astype(F32)).astype(BF)


def turn(a):
    return 2 - a + 3 * (a // 2) - 2 * ((a + 1) // 4)


def kernel(
    users_in, conf_in, lists_in, counts_in, reqs_in, hot_in, cold_in,
    hot_out, cold_out,
    users, conf, lists, counts, reqs, hot, cold, users_t, stack, lmat, cmat, pick, place,
    send0, recv0, spread, first_send, first_recv, gram2,
    csend, crecv,
    sib_out, sib_in, hsend, hrecv, hdir, scal,
    q_part, q_in, q_sum, q_recv,
    cold_sol, cold_res, cold_dir, cold_image,
    insem, sem0, csem, sibsem, hsem, fsem, qsem,
):
    w = lax.axis_index("wide")
    y = lax.axis_index("narrow")
    z = w // 8
    x = (w // 2) % 4
    k = w % 2
    me = w * 4 + y
    chip = (z * 4 + x) * 4 + y
    sibling = (w + 1 - 2 * k, y)

    ys = [lax.rem(y + d, 4) for d in (2, 1, 3, 0)]

    def each_chip(fn):
        def planes(a, carry):
            z2 = lax.rem(z + turn(a), 4)

            def rows(b, inner):
                zx = z2 * 4 + lax.rem(x + turn(b), 4)
                here = jnp.logical_and(a == 3, b == 3)
                for place_at, y2 in enumerate(ys):
                    fn(zx, y2, here if place_at == 3 else None)
                return inner

            return lax.fori_loop(0, 4, rows, carry)

        lax.fori_loop(0, 4, planes, 0)

    def each_other(fn):
        def both_cores(zx, y2, here):
            for core in (1 - k, k):
                w2 = zx * 2 + core
                if here is None or core is not k:
                    fn((w2, y2), w2 * 4 + y2)
                else:
                    pl.when(jnp.logical_not(here))(lambda: fn((w2, y2), w2 * 4 + y2))

        each_chip(both_cores)

    def each_same_core(fn):
        def one(zx, y2, here):
            if here is None:
                fn((zx * 2 + k, y2), zx * 4 + y2)
            else:
                pl.when(jnp.logical_not(here))(lambda: fn((zx * 2 + k, y2), zx * 4 + y2))

        each_chip(one)

    def loop(count, fn, unroll=1):
        def step(t, carry):
            fn(t)
            return carry

        lax.fori_loop(0, count, step, 0, unroll=unroll)

    def push(src, dst, send, recv, device):
        pltpu.make_async_remote_copy(
            src_ref=src, dst_ref=dst, send_sem=send, recv_sem=recv,
            device_id=device, device_id_type=MESH,
        ).start()

    def wait(ref, sem):
        pltpu.make_async_copy(ref, ref, sem).wait()

    loads = [
        pltpu.make_async_copy(src, dst, insem.at[i])
        for i, (src, dst) in enumerate(
            (
                (users_in, users), (conf_in, conf), (hot_in, hot), (cold_in, cold),
                (reqs_in, reqs), (lists_in, lists), (counts_in, counts),
            )
        )
    ]
    for load in loads:
        load.start()
    barrier = pltpu.get_barrier_semaphore()

    def greet(device, _):
        pl.semaphore_signal(barrier, inc=1, device_id=device, device_id_type=MESH)

    each_other(greet)

    loads[4].wait()
    owner_of = lax.broadcasted_iota(jnp.int32, (NDEV, COLD), 0)
    entry = lax.broadcasted_iota(jnp.int32, (NDEV, COLD), 1)
    mine = jnp.where((entry >> 2) == owner_of, reqs[...].astype(F32), 0.0)
    lanes_of = (
        (lax.broadcasted_iota(jnp.int32, (COLD, 128), 0) & 3)
        == lax.broadcasted_iota(jnp.int32, (COLD, 128), 1)
    )
    lane_pick = lanes_of.astype(F32).astype(BF)
    high, low = halves(mine)
    asked = dot(high, lane_pick) + dot(low, lane_pick)
    send0[:, 0:1, :] = asked.reshape(NDEV, 1, 128)
    loads[0].wait()
    for b in range(BLOCKS):
        users_t[:, b * 128:(b + 1) * 128] = users[b * 128:(b + 1) * 128, :].T
    send0[:, 1:2, :] = dot(users_t[...], users[...]).reshape(NDEV, 1, 128)
    loads[1].wait()
    loads[5].wait()
    loads[6].wait()

    def fold(b, first, last, shift):
        listed = lists[pl.ds(b, 1), :]
        column = pl.ds(pl.multiple_of(b * 128, 128), 128)
        row = lax.broadcasted_iota(jnp.int32, (ROWS, LENGTH), 0).astype(F32).astype(BF)
        for base in range(first, last, ROWS):
            near = jnp.clip(listed - base, -1, ROWS).astype(F32).astype(BF)
            chosen = jnp.where(row == near, jnp.ones((), BF), jnp.zeros((), BF))
            both = dot(chosen, stack[b])
            level_sum = both[:, :128]
            lmat[base:base + ROWS, column] = level_sum.astype(BF)
            cmat[base:base + ROWS, column] = (level_sum - both[:, 128:] + shift).astype(BF)

    def fold_hot(b):
        used = lax.broadcasted_iota(jnp.int32, (LENGTH, 128), 0) < counts[b]
        level = jnp.where(used, conf[b].T.astype(F32), 0.0)
        clicked = jnp.where(level > 0.0, 1.0, 0.0)
        stack[b, :, :128] = level.astype(BF)
        stack[b, :, 128:] = clicked.astype(BF)
        fold(b, 0, HOT, 1.0)

    def fold_cold(b):
        fold(b, HOT, TABLE, 0.0)

    loop(EARLY, fold_hot, unroll=2)
    pl.semaphore_wait(barrier, NDEV - 1)

    def send_request(device, s2):
        push(send0.at[s2], recv0.at[me], sem0.at[0], sem0.at[1], device)

    each_other(send_request)
    recv0[pl.ds(me, 1)] = send0[pl.ds(me, 1)]

    def fold_late(b):
        fold_hot(b + EARLY)

    loop(BLOCKS - EARLY, fold_late, unroll=2)
    loop(COLD_EARLY, fold_cold, unroll=4)

    def cold_exchange(e, rows):
        csend[e] = rows.reshape(NDEV, CAP, 128)

        def go(device, s2):
            push(csend.at[e, s2], crecv.at[e, me], csem.at[e, 0], csem.at[e, 1], device)

        each_other(go)
        crecv[e, pl.ds(me, 1)] = csend[e, pl.ds(me, 1)]

    def cold_arrived(e):
        wait(crecv.at[e, pl.ds(0, NDEV - 1)], csem.at[e, 1])
        return crecv[e].reshape(COLD, 128)

    def cold_fetch(e, values):
        cold_exchange(e, dot(pick[...], values.astype(BF)))

    def cold_placed(e):
        high, low = halves(cold_arrived(e))
        both = dot(place[...], jnp.concatenate([high, low], axis=1))
        return both[:, :128] + both[:, 128:]

    def user_terms(table, base, opening):
        rows = pl.ds(base, HALF)
        total = jnp.zeros((HALF, RANK), F32)
        for at in range(0, USERS, PIECE):
            scores = dot(table, users_t[:, at:at + PIECE])
            weight = cmat[rows, at:at + PIECE].astype(F32) * scores
            if opening:
                weight = lmat[rows, at:at + PIECE].astype(F32) - weight
            total = total + dot(weight.astype(BF), users[at:at + PIECE, :])
        return total

    def user_squares(table, base):
        rows = pl.ds(base, HALF)
        total = jnp.zeros((HALF, 128), F32)
        for at in range(0, USERS, PIECE):
            scores = dot(table, users_t[:, at:at + PIECE])
            part = cmat[rows, at:at + PIECE].astype(F32) * scores * scores
            for lane in range(0, PIECE, 128):
                total = total + part[:, lane:lane + 128]
        return total

    other_base = (1 - k) * HALF
    own_base = k * HALF

    def hot_give_sibling(g, read_table, opening):
        base = pl.multiple_of(other_base, HALF)
        sib_out[g] = user_terms(read_table(base), base, opening)
        push(sib_out.at[g], sib_in.at[g], sibsem.at[g, 0], sibsem.at[g, 1], sibling)

    def hot_give_own(g, read_table, opening):
        base = pl.multiple_of(own_base, HALF)
        hsend[g] = user_terms(read_table(base), base, opening)

    def hot_give(g):
        wait(sib_in.at[g], sibsem.at[g, 1])
        hsend[g] = hsend[g] + sib_in[g]

        def go(device, c2):
            push(
                hsend.at[g, pl.ds(pl.multiple_of(c2 * OWN, OWN), OWN)], hrecv.at[g, chip],
                hsem.at[g, 0], hsem.at[g, 1], device,
            )

        each_same_core(go)
        hrecv[g, pl.ds(chip, 1)] = hsend[
            g, pl.ds(pl.multiple_of(chip * OWN, OWN), OWN), :
        ].reshape(1, OWN, 128)

    def hot_given(g):
        wait(hrecv.at[g, pl.ds(0, NCHIP - 1)], hsem.at[g, 1])
        return jnp.sum(hrecv[g], axis=0)

    own_rows = pl.ds(pl.multiple_of(own_base + chip * OWN, OWN), OWN)
    own_half = pl.ds(pl.multiple_of(own_base, HALF), HALF)

    def hot_spread(buf, f, values):
        buf[own_rows, :] = values

        def go(device, _):
            push(buf.at[own_rows], buf.at[own_rows], fsem.at[f, 0], fsem.at[f, 1], device)

        each_same_core(go)

    def hot_forward(buf, f):
        wait(buf.at[pl.ds(0, (NCHIP - 1) * OWN)], fsem.at[f, 1])
        push(buf.at[own_half], buf.at[own_half], fsem.at[f, 2], fsem.at[f, 3], sibling)

    def hot_forwarded(buf, f):
        wait(buf.at[pl.ds(0, HALF)], fsem.at[f, 3])

    def read_rows(buf):
        return lambda base: buf[pl.ds(base, HALF), :].astype(BF)

    def cold_give(e, table, opening):
        cold_exchange(e, user_terms(table.astype(BF), HOT, opening))

    def apply_gram(v):
        high, low = halves(v)
        return dot(high, gram2[0]) + dot(high, gram2[1]) + dot(low, gram2[0]) + REGULAR * v

    def row_sum(v):
        return jnp.sum(v, axis=1, keepdims=True)

    spread[...] = (
        (lax.broadcasted_iota(jnp.int32, (COLD, NDEV), 0) >> 2)
        == lax.broadcasted_iota(jnp.int32, (COLD, NDEV), 1)
    ).astype(F32).astype(BF)
    wait(recv0.at[pl.ds(0, NDEV - 1)], sem0.at[1])
    gram_row = jnp.sum(recv0[:, 1:2, :], axis=0, keepdims=True)
    first_send[:, CAP:, :] = jnp.broadcast_to(gram_row, (NDEV, 1, 128))
    high, low = halves(recv0[:, 0:1, :].reshape(NDEV, 128))
    rows4 = jnp.where(lanes_of, dot(spread[...], high) + dot(spread[...], low), 0.0)
    wanted_col = row_sum(rows4).astype(jnp.int32)
    lane_item = lax.broadcasted_iota(jnp.int32, (COLD, COLD), 1)
    pick[...] = jnp.where(wanted_col == lane_item, 1.0, 0.0).astype(BF)
    loads[3].wait()
    first_send[:, 0:CAP, :] = dot(pick[...], cold[...].astype(BF)).reshape(NDEV, CAP, 128)

    def send_first(device, s2):
        push(first_send.at[s2], first_recv.at[me], csem.at[0, 0], csem.at[0, 1], device)

    each_other(send_first)
    first_recv[pl.ds(me, 1)] = first_send[pl.ds(me, 1)]
    wanted_wide = jnp.broadcast_to(wanted_col, (COLD, 128))
    wanted_row = wanted_wide.astype(F32).T[0:1, :].astype(jnp.int32)
    row_item = lax.broadcasted_iota(jnp.int32, (COLD, COLD), 0)
    place[...] = jnp.where(wanted_row == row_item, 1.0, 0.0).astype(BF)

    loads[2].wait()
    hot_give_sibling(0, read_rows(hot), True)
    hot_give_own(0, read_rows(hot), True)
    hot_give(0)
    loop(BLOCKS - COLD_EARLY, lambda b: fold_cold(b + COLD_EARLY), unroll=4)

    wait(first_recv.at[pl.ds(0, NDEV - 1)], csem.at[0, 1])
    cold_give(1, first_recv[:, 0:CAP, :].reshape(COLD, 128), True)

    gram2[0], gram2[1] = halves(first_recv[:, CAP:, :].reshape(RANK, RANK))
    cold_image[...] = apply_gram(cold[...])
    hot_res = hot_given(0) - REGULAR * hot[own_rows, :]
    hot_dir = hot_res
    hot_norm = row_sum(hot_res * hot_res)
    hdir0 = hdir.at[0]
    hdir1 = hdir.at[1]
    hot_spread(hdir0, 0, hot_dir)

    residual = cold_placed(1) - cold_image[...]
    cold_res[...] = residual
    cold_fetch(2, residual)
    cold_norm = row_sum(residual * residual)
    cold_image[...] = apply_gram(residual)
    cold_curve = row_sum(residual * cold_image[...])

    hot_forward(hdir0, 0)
    hot_give_own(1, read_rows(hdir0), False)
    hot_forwarded(hdir0, 0)
    hot_give_sibling(1, read_rows(hdir0), False)
    hot_give(1)
    cold_give(3, cold_arrived(2), False)

    image = hot_given(1) + REGULAR * hot_dir
    hot_alpha = hot_norm / (row_sum(hot_dir * image) + EPS)
    hot_res = hot_res - hot_alpha * image
    fresh = row_sum(hot_res * hot_res)
    hot_dir = hot_res + fresh / (hot_norm + EPS) * hot_dir
    hot_spread(hdir1, 1, hot_dir)
    lane = lax.broadcasted_iota(jnp.int32, (OWN, 128), 1)
    scal_own = jnp.where(lane < 64, hot_alpha, fresh)

    term = cold_placed(3)
    old = cold_res[...]
    cold_alpha = cold_norm / (row_sum(old * term) + cold_curve + EPS)
    residual = old - cold_alpha * (term + cold_image[...])
    fresh = row_sum(residual * residual)
    direction = residual + fresh / (cold_norm + EPS) * old
    cold_fetch(4, direction)
    cold_sol[...] = cold[...] + cold_alpha * old
    cold_dir[...] = direction
    cold_norm = fresh
    cold_curve = row_sum(direction * apply_gram(direction))
    hot_spread(scal, 2, scal_own)

    hot_forward(hdir1, 1)

    def hot_squares(base):
        start = pl.multiple_of(base, HALF)
        square = user_squares(hdir[1, pl.ds(start, HALF), :].astype(BF), start)
        for j in range(HALF // 128):
            q_part[pl.ds(start // 128 + j, 1), :] = jnp.sum(
                square[j * 128:(j + 1) * 128, :].T, axis=0, keepdims=True
            )

    hot_squares(own_base)
    hot_forwarded(hdir1, 1)
    hot_squares(other_base)
    push(q_part, q_in, qsem.at[0], qsem.at[1], sibling)
    wait(q_in, qsem.at[1])
    q_sum[...] = q_part[...] + q_in[...]

    def send_q(device, _):
        push(q_sum, q_recv.at[chip], qsem.at[2], qsem.at[3], device)

    each_same_core(send_q)
    q_recv[pl.ds(chip, 1)] = q_sum[...].reshape(1, OWN, 128)

    cold_exchange(5, user_squares(cold_arrived(4).astype(BF), HOT))

    hot_forward(scal, 2)
    hot_forwarded(scal, 2)
    curves = []
    for a in range(HOT // 128):
        rows = slice(a * 128, (a + 1) * 128)
        d1 = hdir[1, rows, :]
        curves.append(REGULAR * row_sum(d1 * d1) + EPS)
        hot_out[rows, :] = hot[rows, :] + scal[rows, 0:1] * hdir[0, rows, :]
    wait(q_recv.at[pl.ds(0, NCHIP - 1)], qsem.at[3])
    q_col = jnp.sum(q_recv[...], axis=0).T
    for a in range(HOT // 128):
        rows = slice(a * 128, (a + 1) * 128)
        alpha = scal[rows, 64:65] / (q_col[:, a:a + 1] + curves[a])
        hot_out[rows, :] = hot_out[rows, :] + alpha * hdir[1, rows, :]

    wait(send0.at[pl.ds(0, NDEV - 1)], sem0.at[0])

    wait(first_send.at[pl.ds(0, NDEV - 1)], csem.at[0, 0])
    for e in range(1, 5):
        wait(csend.at[e, pl.ds(0, NDEV - 1)], csem.at[e, 0])
    for g in range(2):
        wait(sib_out.at[g], sibsem.at[g, 0])
        wait(hrecv.at[g, pl.ds(0, NCHIP - 1)], hsem.at[g, 0])
    for f in range(3):
        wait(hrecv.at[0, pl.ds(0, NCHIP - 1)], fsem.at[f, 0])
        wait(scal.at[pl.ds(0, HALF)], fsem.at[f, 2])
    wait(q_part, qsem.at[0])
    wait(q_recv.at[pl.ds(0, NCHIP - 1)], qsem.at[2])

    alpha = cold_norm / (row_sum(cold_placed(5)) + cold_curve + EPS)
    cold_out[...] = cold_sol[...] + alpha * cold_dir[...]
    wait(csend.at[5, pl.ds(0, NDEV - 1)], csem.at[5, 0])


def hand_over(hot_in, cold_in, hot_out, cold_out):
    hot_out[...] = hot_in[...]
    cold_out[...] = cold_in[...]


def body(users, confidence, item_lists, block_counts, requests, hot_factors, cold_factors):
    hbm = pl.BlockSpec(memory_space=pl.ANY)
    dma = pltpu.SemaphoreType.DMA
    outs = (
        jax.ShapeDtypeStruct((HOT, RANK), F32),
        jax.ShapeDtypeStruct((COLD, RANK), F32),
    )
    vmem = pl.BlockSpec(memory_space=pltpu.VMEM)
    results = pl.pallas_call(
        kernel,
        out_shape=(pltpu.VMEM((HOT, RANK), F32), pltpu.VMEM((COLD, RANK), F32)),
        in_specs=[hbm] * 7,
        out_specs=(vmem, vmem),
        scratch_shapes=[
            pltpu.VMEM((USERS, RANK), BF),
            pltpu.VMEM((BLOCKS, 128, LENGTH), BF),
            pltpu.VMEM((BLOCKS, LENGTH), jnp.int32),
            pltpu.SMEM((BLOCKS,), jnp.int32),
            pltpu.VMEM((1, COLD), jnp.int32),
            pltpu.VMEM((HOT, RANK), F32),
            pltpu.VMEM((COLD, RANK), F32),
            pltpu.VMEM((RANK, USERS), BF),
            pltpu.VMEM((BLOCKS, LENGTH, 256), BF),
            pltpu.VMEM((TABLE, USERS), BF),
            pltpu.VMEM((TABLE, USERS), BF),
            pltpu.VMEM((COLD, COLD), BF),
            pltpu.VMEM((COLD, COLD), BF),
            pltpu.VMEM((NDEV, 2, 128), F32),
            pltpu.VMEM((NDEV, 2, 128), F32),
            pltpu.VMEM((COLD, NDEV), BF),
            pltpu.VMEM((NDEV, CAP + 1, 128), F32),
            pltpu.VMEM((NDEV, CAP + 1, 128), F32),
            pltpu.VMEM((2, RANK, RANK), BF),
            pltpu.VMEM((6, NDEV, CAP, 128), F32),
            pltpu.VMEM((6, NDEV, CAP, 128), F32),
            pltpu.VMEM((2, HALF, 128), F32),
            pltpu.VMEM((2, HALF, 128), F32),
            pltpu.VMEM((2, HALF, 128), F32),
            pltpu.VMEM((2, NCHIP, OWN, 128), F32),
            pltpu.VMEM((2, HOT, 128), F32),
            pltpu.VMEM((HOT, 128), F32),
            pltpu.VMEM((OWN, 128), F32),
            pltpu.VMEM((OWN, 128), F32),
            pltpu.VMEM((OWN, 128), F32),
            pltpu.VMEM((NCHIP, OWN, 128), F32),
            pltpu.VMEM((COLD, RANK), F32),
            pltpu.VMEM((COLD, RANK), F32),
            pltpu.VMEM((COLD, RANK), F32),
            pltpu.VMEM((COLD, RANK), F32),
            dma((7,)),
            dma((2,)),
            dma((6, 2)),
            dma((2, 2)),
            dma((2, 2)),
            dma((3, 4)),
            dma((4,)),
        ],
        compiler_params=pltpu.CompilerParams(
            collective_id=0, has_side_effects=True, vmem_limit_bytes=58 << 20
        ),
    )(users, confidence, item_lists, block_counts, requests, hot_factors, cold_factors)
    return pl.pallas_call(
        hand_over,
        out_shape=outs,
        in_specs=[vmem, vmem],
        out_specs=(vmem, vmem),
    )(*(pltpu.with_memory_space_constraint(r, pltpu.VMEM) for r in results))


def solution(mesh):
    both = ("wide", "narrow")
    placed = (
        P(both, None),
        P(both, None, None),
        P(both, None),
        P(both),
        P(both, None),
        P(),
        P(both, None),
    )
    return jax.shard_map(
        body,
        mesh=mesh,
        in_specs=placed,
        out_specs=(P(), P(both, None)),
        check_vma=False,
    )
```
